128 devices in a mesh: row: 8 (over z, core), col: 16 (over y, x).
Axes of the slice: x: 4, y: 4, z: 4, core: 2. Of those that a mesh axis runs over, the one named last changes fastest.
Arguments:
- amplitudes: float32 [1024, 16384], P('col', 'row'), may hold values from -6 to 6
- integrals: float32 [16384, 32768], P('row', 'col'), may hold values from -0.046875 to 0.046875
- integral_mask: int32 [128, 256], P('row', 'col'), may hold values 0 or 1
- denominators: float32 [1024, 32768], P('row', 'col'), may hold values from 0.25 to 2
- cycle_tiles: float32 [32768, 512], P('col'), may hold values from -0.25 to 0.25
- cycle_mask: int32 [256, 4], P('col'), may hold values 0 or 1
- destination: int32 [1024, 256], P('row', 'col'), may hold values from 0 to 262143, as said below
Outputs:
- update: float32 [1024, 32768], P('row', 'col')
- cycle_term: float32 [1024, 32768], P('row', 'col')
The draws below stay inside these ranges and needn't reach their ends.
Inputs may be any that keep to these rules, and one draw needn't show every extreme that they name: destination is a permutation of the units. Numbering a unit (r, t) as r * 256 + t and cutting the units into blocks of 128 rows by 16 tiles, every block sends exactly 16 of its units to every block.
All inputs are finite; a program needn't handle non-finite values. No bound on the sum of `integral_mask` or of `cycle_mask` on one device may be relied on, other than what follows from the above.
Results may differ from the reference program's by a relative error of at most 0.0003.
Values sent between devices are 32-bit elements; how exact they have to be, the bound alone decides.
No kernel may reach another device: no remote copies, remote signals or barrier semaphores. Data moves between devices by JAX's collectives and lax.ppermute only.
A program may use at most 128 MiB of HBM per device.

```python
import math
import jax
import jax.numpy as jnp
from jax import lax

V2 = 32768
TILE = 128
RB = 512
OCC = 1024
VT = 256
CD = 16384
IJ_DEV = 128
TPD = 16
CAP = 16


def draw_destination(key, part):
    base = jax.random.fold_in(key, 7)
    key_src, key_dst = jax.random.split(base)
    units = IJ_DEV * TPD
    row_blocks = OCC // IJ_DEV
    col_blocks = VT // TPD
    ndev = row_blocks * col_blocks
    src_perm = jax.vmap(lambda k: jax.random.permutation(k, units))(jax.random.split(key_src, ndev)).astype(jnp.int32)
    dst_perm = jax.vmap(lambda k: jax.random.permutation(k, units))(jax.random.split(key_dst, ndev)).astype(jnp.int32)
    dvec = jnp.arange(ndev, dtype=jnp.int32)[:, None, None]
    svec = jnp.arange(ndev, dtype=jnp.int32)[None, :, None]
    kvec = jnp.arange(CAP, dtype=jnp.int32)[None, None, :]
    slot = dst_perm[dvec, svec * CAP + kvec]
    local = src_perm[svec, dvec * CAP + kvec]

    def global_unit(device, loc):
        prow = device // col_blocks
        pcol = device % col_blocks
        return (prow * IJ_DEV + loc // TPD) * VT + pcol * TPD + loc % TPD
    out_q = global_unit(jnp.broadcast_to(dvec, slot.shape), slot)
    in_q = global_unit(jnp.broadcast_to(svec, local.shape), local)
    dest = jnp.zeros((OCC * VT,), jnp.int32).at[in_q.reshape(-1)].set(out_q.reshape(-1))
    return dest.reshape(OCC, VT)


def touch_ends(values, own_key, smallest, top_value):
    shape = values.shape
    spot = [jax.random.randint(jax.random.fold_in(own_key, axis), (), 0, shape[axis]) for axis in range(len(shape))]
    values = values.at[tuple(spot)].set(smallest)
    longest = shape.index(max(shape))
    spot[longest] = (spot[longest] + 1) % shape[longest]
    return values.at[tuple(spot)].set(top_value)


def level_of(rng, dims, cuts, low, largest):
    def one(axis_at, parts):
        draws = jax.random.uniform(jax.random.fold_in(jax.random.fold_in(rng, 6), axis_at), (parts,), jnp.float32, low / len(cuts), largest / len(cuts))
        return jnp.repeat(jnp.exp(draws), dims[axis_at] // parts).reshape((-1,) + (1,) * (len(dims) - axis_at - 1))

    loudness = one(*cuts[0])
    for cut in cuts[1:]:
        loudness = loudness * one(*cut)
    return loudness


def gaussian(rng, dims, deviation, most, cuts=(), kind=jnp.bfloat16):
    level = level_of(rng, dims, cuts, -0.22, 0.18) if cuts else 1.0
    array = jax.random.normal(rng, dims, jnp.float32) * deviation * level
    return jnp.minimum(jnp.maximum(array, -most), most).astype(kind)


def setup_inputs(seed: int = 0) -> dict:
    key_list = jax.random.split(jax.random.key(seed), 8)
    return {
        "amplitudes": gaussian(key_list[0], (OCC, CD), 1.0, 6.0, ((0, 16), (1, 8)), jnp.float32),
        "integrals": gaussian(key_list[1], (CD, V2), CD ** -0.5, 0.046875, ((0, 8), (1, 16)), jnp.float32),
        "integral_mask": touch_ends((jax.random.randint(key_list[2], (CD // TILE, VT), 0, 5) < 3).astype(jnp.int32), jax.random.fold_in(key_list[2], 1), 0, 1),
        "denominators": jnp.clip(jnp.exp(math.log(2.0) - 2.0794415 * jax.random.uniform(key_list[3], (OCC, V2), jnp.float32) ** level_of(key_list[3], (OCC, V2), ((0, 8), (1, 16)), -0.2, 0.2)), 0.25, 2.0),
        "cycle_tiles": gaussian(key_list[4], (V2, RB), RB ** -0.5, 0.25, ((0, 16),), jnp.float32),
        "cycle_mask": touch_ends((jax.random.randint(key_list[5], (VT, RB // TILE), 0, 5) < 3).astype(jnp.int32), jax.random.fold_in(key_list[5], 1), 0, 1),
        "destination": draw_destination(jax.random.fold_in(key_list[7], 71), 0),
    }


def reference(amplitudes, integrals, integral_mask, denominators, cycle_tiles, cycle_mask, destination):
    width = V2 // 16
    tiles_blk = width // TILE
    mask_f = integral_mask.astype(jnp.float32)

    def column_block(index):
        start = (index * width).astype(jnp.int32)
        block = lax.dynamic_slice_in_dim(integrals, start, width, 1)
        mblock = lax.dynamic_slice_in_dim(mask_f, (index * tiles_blk).astype(jnp.int32), tiles_blk, 1)
        masked = (block.reshape(CD // TILE, TILE, tiles_blk, TILE) * mblock[:, None, :, None]).reshape(CD, width)
        return jnp.dot(amplitudes, masked, precision=lax.Precision.HIGHEST, preferred_element_type=jnp.float32)

    blocks = lax.map(column_block, jnp.arange(16, dtype=jnp.int32))
    residual = jnp.transpose(blocks, (1, 0, 2)).reshape(OCC, V2)
    units = residual.reshape(OCC * VT, TILE)
    moved = jnp.zeros_like(units).at[destination.reshape(-1)].set(units).reshape(OCC, V2)
    update = moved / denominators
    rmask = cycle_mask.astype(jnp.float32)
    cycle = (cycle_tiles.reshape(VT, TILE, RB // TILE, TILE) * rmask[:, None, :, None]).reshape(V2 // RB, RB, RB)
    cycle_term = jnp.einsum("okr,krs->oks", update.reshape(OCC, V2 // RB, RB), cycle,
                           precision=lax.Precision.HIGHEST, preferred_element_type=jnp.float32).reshape(OCC, V2)
    return update, cycle_term
```

```python
import functools

import jax
import jax.numpy as jnp
from jax import lax
from jax.experimental import pallas as pl
from jax.experimental.pallas import tpu as pltpu
from jax.sharding import Mesh, PartitionSpec as P

TILE = 128
RB = 512
VT = 256
ROWS = 128
TPD = 16
CAP = 16
NZ = 4
SPLITS = (32, 32)
NB = 256
MIB = 1 << 20

f32 = jnp.float32
bf16 = jnp.bfloat16


def split(x):
    hi = x.astype(bf16)
    return hi, (x - hi.astype(f32)).astype(bf16)


def call(kernel, out_shape, *, vmem=48, flops=0, nbytes=0, **kw):
    return pl.pallas_call(
        kernel,
        out_shape=out_shape,
        compiler_params=pltpu.CompilerParams(vmem_limit_bytes=vmem * MIB),
        cost_estimate=pl.CostEstimate(flops=flops, bytes_accessed=nbytes, transcendentals=0),
        **kw,
    )


def prep_kernel(mask_ref, x_ref, hi_ref, lo_ref, *, tile_rows, tile_cols, step_axis):
    step = pl.program_id(0)
    for i in range(tile_rows):
        for j in range(tile_cols):
            mi = i + (step * tile_rows if step_axis == 0 else 0)
            mj = j + (step * tile_cols if step_axis == 1 else 0)
            m = mask_ref[mi, mj].astype(f32)
            sl = (slice(i * TILE, (i + 1) * TILE), slice(j * TILE, (j + 1) * TILE))
            hi, lo = split(x_ref[sl] * m)
            hi_ref[sl] = hi
            lo_ref[sl] = lo


def prep(x, mask, block, step_axis):
    rows, cols = x.shape
    grid = (rows // block[0],) if step_axis == 0 else (cols // block[1],)
    imap = (lambda n: (n, 0)) if step_axis == 0 else (lambda n: (0, n))
    spec = pl.BlockSpec(block, imap)
    out = jax.ShapeDtypeStruct((rows, cols), bf16)
    return call(
        functools.partial(prep_kernel, tile_rows=block[0] // TILE, tile_cols=block[1] // TILE, step_axis=step_axis),
        (out, out),
        grid=grid,
        in_specs=[pl.BlockSpec(memory_space=pltpu.SMEM), spec],
        out_specs=(spec, spec),
        nbytes=rows * cols * 8,
        flops=rows * cols * 4,
    )(mask, x)


def mm_kernel(order_ref, a_ref, bh_ref, bl_ref, o_ref, ah, al, *, sub):
    @pl.when(pl.program_id(0) == 0)
    def _():
        for i in range(NZ):
            r = order_ref[i]
            for j in range(2):
                hi, lo = split(a_ref[2 * r + j])
                at = slice((2 * i + j) * sub, (2 * i + j + 1) * sub)
                ah[at, :] = hi
                al[at, :] = lo

    dot = functools.partial(jnp.dot, preferred_element_type=f32)
    acc = dot(ah[...], bh_ref[...]) + dot(ah[...], bl_ref[...]) + dot(al[...], bh_ref[...])
    for i in range(NZ):
        for t in range(NB // TILE):
            o_ref[i, t] = acc[2 * sub * i : 2 * sub * (i + 1), t * TILE : (t + 1) * TILE]


def multiply(a, bh, bl, order, part):
    sub = SPLITS[part]
    assert sum(SPLITS[:part]) % sub == 0
    at = sum(SPLITS[:part]) // sub
    depth, cols = bh.shape
    m = NZ * 2 * sub
    return call(
        functools.partial(mm_kernel, sub=sub),
        jax.ShapeDtypeStruct((NZ, cols // TILE, 2 * sub, TILE), f32),
        grid=(cols // NB,),
        in_specs=[
            pl.BlockSpec(memory_space=pltpu.SMEM),
            pl.BlockSpec((16, sub, depth), lambda n: (0, at, 0)),
            pl.BlockSpec((depth, NB), lambda n: (0, n)),
            pl.BlockSpec((depth, NB), lambda n: (0, n)),
        ],
        out_specs=pl.BlockSpec((NZ, NB // TILE, 2 * sub, TILE), lambda n: (0, n, 0, 0)),
        scratch_shapes=[pltpu.VMEM((m, depth), bf16), pltpu.VMEM((m, depth), bf16)],
        flops=6 * m * depth * cols,
        nbytes=4 * depth * cols + 4 * m * cols,
    )(order, a, bh, bl)


def far_kernel(mine_ref, got_ref, p_ref, m_ref):
    half = TPD // 2
    p_ref[...] = mine_ref[0, :half] + got_ref[0, :half]
    m_ref[...] = mine_ref[0, half:] + got_ref[0, half:]


def far(mine, got):
    block = (1,) + mine.shape[1:]
    shape = jax.ShapeDtypeStruct((TPD // 2,) + mine.shape[2:], f32)
    spec = pl.BlockSpec(block, lambda n: (0, 0, 0, 0))
    whole = pl.BlockSpec(shape.shape, lambda n: (0, 0, 0))
    return call(far_kernel, (shape, shape), grid=(1,), in_specs=[spec, spec], out_specs=(whole, whole), nbytes=3 * 1024 * 512)(mine, got)


def near_kernel(mine_ref, got_ref, gp_ref, gm_ref, p_ref, m_ref):
    half = TPD // 2
    p_ref[:half] = mine_ref[0, :half] + got_ref[0, :half] + gp_ref[...]
    p_ref[half:] = mine_ref[0, half:] + got_ref[0, half:]
    m_ref[:half] = mine_ref[1, :half] + got_ref[1, :half]
    m_ref[half:] = mine_ref[1, half:] + got_ref[1, half:] + gm_ref[...]


def near(mine, got, gp, gm):
    rows = mine.shape[2]
    two = pl.BlockSpec((pl.Element(2), pl.Element(TPD), pl.Element(rows), pl.Element(TILE)), lambda n: (1, 0, 0, 0))
    part = pl.BlockSpec(gp.shape, lambda n: (0, 0, 0))
    shape = jax.ShapeDtypeStruct(mine.shape[1:], f32)
    whole = pl.BlockSpec(shape.shape, lambda n: (0, 0, 0))
    return call(near_kernel, (shape, shape), grid=(1,), in_specs=[two, two, part, part], out_specs=(whole, whole), nbytes=7 * 1024 * 512)(mine, got, gp, gm)


def gather_kernel(idx_ref, *refs):
    ins, (out_ref, scr) = refs[:-2], refs[-2:]
    base = 0
    for c in range(len(SPLITS)):
        mine, got, rp, rm = ins[4 * c : 4 * c + 4]
        rows = 2 * SPLITS[c]
        for t in range(TPD):
            scr[base + t * rows : base + (t + 1) * rows, :] = mine[0, t] + got[0, t] + rp[t] + rm[t]
        base += TPD * rows

    def step(g, carry):
        for k in range(16):
            i = g * 16 + k
            out_ref[pl.ds(i, 1), :] = scr[pl.ds(idx_ref[i], 1), :]
        return carry

    lax.fori_loop(0, ROWS * TPD // 16, step, 0)


def gather(idx, parts):
    units = ROWS * TPD
    specs = [pl.BlockSpec(memory_space=pltpu.SMEM)]
    flat = []
    for mine, got, rp, rm in parts:
        own = pl.BlockSpec((1,) + mine.shape[1:], lambda n: (NZ - 1, 0, 0, 0))
        whole = pl.BlockSpec(rp.shape, lambda n: (0, 0, 0))
        specs += [own, own, whole, whole]
        flat += [mine, got, rp, rm]
    return call(
        gather_kernel,
        jax.ShapeDtypeStruct((units, TILE), f32),
        grid=(1,),
        in_specs=specs,
        out_specs=pl.BlockSpec((units, TILE), lambda n: (0, 0)),
        scratch_shapes=[pltpu.VMEM((units, TILE), f32)],
        nbytes=5 * units * TILE * 4,
    )(idx, *flat)


def finish_kernel(place_ref, got_ref, den_ref, ch_ref, cl_ref, up_ref, ct_ref, scr):
    def step(g, carry):
        for k in range(16):
            i = g * 16 + k
            scr[pl.ds(place_ref[i], 1), :] = got_ref[pl.ds(i, 1), :]
        return carry

    lax.fori_loop(0, ROWS * TPD // 16, step, 0)
    for t in range(TPD):
        at = slice(t * TILE, (t + 1) * TILE)
        up_ref[:, at] = scr[at, :] / den_ref[:, at]
    dot = functools.partial(jnp.dot, preferred_element_type=f32)
    for k in range(TPD * TILE // RB):
        at = slice(k * RB, (k + 1) * RB)
        hi, lo = split(up_ref[:, at])
        ct_ref[:, at] = dot(hi, ch_ref[at, :]) + dot(hi, cl_ref[at, :]) + dot(lo, ch_ref[at, :])


def finish(place, got, den, ch, cl):
    shape = jax.ShapeDtypeStruct(den.shape, f32)
    whole = lambda s: pl.BlockSpec(s, lambda n: (0, 0))
    return call(
        finish_kernel,
        (shape, shape),
        grid=(1,),
        in_specs=[pl.BlockSpec(memory_space=pltpu.SMEM), whole(got.shape), whole(den.shape), whole(ch.shape), whole(cl.shape)],
        out_specs=(whole(den.shape), whole(den.shape)),
        scratch_shapes=[pltpu.VMEM(got.shape, f32)],
        nbytes=8 << 20,
    )(place, got, den, ch, cl)


def plan(destination):
    flat = destination.reshape(-1)
    out_row = flat // VT
    out_tile = flat % VT
    owner = out_row // ROWS * (VT // TPD) + out_tile // TPD
    place = out_tile % TPD * ROWS + out_row % ROWS
    unit = jnp.arange(ROWS * TPD, dtype=jnp.int32)
    row, tile = unit // TPD, unit % TPD
    block, sub = row // 64, row % 64
    at = jnp.zeros_like(unit)
    first, base = 0, 0
    for rows in SPLITS:
        here = base + tile * (2 * rows) + block * rows + (sub - first)
        at = jnp.where(sub >= first, here, at)
        first += rows
        base += TPD * 2 * rows
    key = lax.sort((owner << 22) | (at << 11) | place)
    return (key >> 11) & 2047, key & 2047


def ring(step):
    return [(i, (i + step) % NZ) for i in range(NZ)]


def body(amplitudes, integrals, integral_mask, denominators, cycle_tiles, cycle_mask, destination):
    everyone = ("z", "core", "y", "x")
    z = lax.axis_index("z")
    core = lax.axis_index("core")
    depth = integrals.shape[0]

    gathered = lax.all_gather(amplitudes, ("y", "x"), axis=0, tiled=True).reshape(16, 64, depth)

    bh, bl = prep(integrals, integral_mask, (depth, NB), 1)
    source, place = plan(destination)
    place = place.astype(f32).reshape(128, 1, CAP)
    got_place = lax.all_to_all(place, everyone, split_axis=0, concat_axis=0, tiled=True)
    got_place = got_place.reshape(-1).astype(jnp.int32)
    ch, cl = prep(cycle_tiles, cycle_mask, (512, RB), 0)
    bh, bl, ch, cl, source, got_place = lax.optimization_barrier((bh, bl, ch, cl, source, got_place))

    towards = jnp.array([2, 1, 3, 0], jnp.int32)
    order = 2 * ((z + towards) % NZ)
    own_order, other_order = order + core, order + (1 - core)

    parts = []
    for c in range(len(SPLITS)):
        theirs = multiply(gathered, bh, bl, other_order, c)
        got = lax.ppermute(theirs, "core", [(0, 1), (1, 0)])
        mine = multiply(gathered, bh, bl, own_order, c)
        far_p, far_m = far(mine, got)
        gp = lax.ppermute(far_p, "z", ring(1))
        gm = lax.ppermute(far_m, "z", ring(-1))
        near_p, near_m = near(mine, got, gp, gm)
        rp = lax.ppermute(near_p, "z", ring(1))
        rm = lax.ppermute(near_m, "z", ring(-1))
        parts.append((mine, got, rp, rm))

    sending = gather(source, parts).reshape(128, CAP, TILE)
    units = lax.all_to_all(sending, everyone, split_axis=0, concat_axis=0, tiled=True)
    return finish(got_place, units.reshape(-1, TILE), denominators, ch, cl)


def solution(mesh):
    row, col = ("z", "core"), ("y", "x")
    split_mesh = Mesh(mesh.devices.reshape(4, 2, 4, 4), row + col)
    return jax.shard_map(
        body,
        mesh=split_mesh,
        in_specs=(P(col, row), P(row, col), P(row, col), P(row, col), P(col, None), P(col, None), P(row, col)),
        out_specs=(P(row, col), P(row, col)),
        check_vma=False,
    )
```

```python
import functools

import jax
import jax.numpy as jnp
from jax import lax
from jax.experimental import pallas as pl
from jax.experimental.pallas import tpu as pltpu
from jax.sharding import Mesh, PartitionSpec as P

TILE = 128
RB = 512
VT = 256
ROWS = 128
TPD = 16
CAP = 16
NZ = 4
PARTS = 2
SUB = 32
COLOURS = 4
NB = 256
MIB = 1 << 20

f32 = jnp.float32
bf16 = jnp.bfloat16


def split(x):
    hi = x.astype(bf16)
    return hi, (x - hi.astype(f32)).astype(bf16)


def call(kernel, out_shape, *, vmem=48, flops=0, nbytes=0, **kw):
    return pl.pallas_call(
        kernel,
        out_shape=out_shape,
        compiler_params=pltpu.CompilerParams(vmem_limit_bytes=vmem * MIB),
        cost_estimate=pl.CostEstimate(flops=flops, bytes_accessed=nbytes, transcendentals=0),
        **kw,
    )


def masked_split(mask_ref, x_ref, mi, mj, i, j):
    m = mask_ref[mi, mj].astype(f32)
    return split(x_ref[i * TILE : (i + 1) * TILE, j * TILE : (j + 1) * TILE] * m)


def cycle_kernel(mask_ref, x_ref, hi_ref, lo_ref):
    for i in range(RB // TILE):
        for j in range(RB // TILE):
            hi, lo = masked_split(mask_ref, x_ref, pl.program_id(0) * (RB // TILE) + i, j, i, j)
            at = (slice(i * TILE, (i + 1) * TILE), slice(j * TILE, (j + 1) * TILE))
            hi_ref[at] = hi
            lo_ref[at] = lo


def prepare_cycle(x, mask):
    spec = pl.BlockSpec((RB, RB), lambda n: (n, 0))
    out = jax.ShapeDtypeStruct(x.shape, bf16)
    return call(
        cycle_kernel,
        (out, out),
        grid=(x.shape[0] // RB,),
        in_specs=[pl.BlockSpec(memory_space=pltpu.SMEM), spec],
        out_specs=(spec, spec),
        nbytes=x.size * 8,
        flops=x.size * 4,
    )(mask, x)


def integrals_kernel(mask_ref, x_ref, *refs, first):
    hi_ref, lo_ref = refs[-2:]
    step = first + pl.program_id(0)
    for i in range(x_ref.shape[0] // TILE):
        for j in range(NB // TILE):
            hi, lo = masked_split(mask_ref, x_ref, i, step * (NB // TILE) + j, i, j)
            at = (0, slice(i * TILE, (i + 1) * TILE), slice(j * TILE, (j + 1) * TILE))
            hi_ref[at] = hi
            lo_ref[at] = lo


def prepare_integrals(x, mask, first, count, into=None):
    depth, cols = x.shape
    out = jax.ShapeDtypeStruct((cols // NB, depth, NB), bf16)
    spec = pl.BlockSpec((1, depth, NB), lambda n: (n + first, 0, 0))
    kw = {}
    specs = [pl.BlockSpec(memory_space=pltpu.SMEM), pl.BlockSpec((depth, NB), lambda n: (0, n + first))]
    extra = ()
    if into is not None:
        extra = into
        specs += [pl.BlockSpec(memory_space=pl.ANY)] * 2
        kw["input_output_aliases"] = {2: 0, 3: 1}
    return call(
        functools.partial(integrals_kernel, first=first),
        (out, out),
        grid=(count,),
        in_specs=specs,
        out_specs=(spec, spec),
        nbytes=depth * NB * 8 * count,
        flops=depth * NB * 4 * count,
        **kw,
    )(mask, x, *extra)


def mm_kernel(where_ref, *refs):
    held, bh_ref, bl_ref, o_ref, ah, al = refs[:-5], *refs[-5:]
    near, late = held[:COLOURS], held[COLOURS:]

    @pl.when(pl.program_id(0) == 0)
    def _():
        for s in range(2 * NZ):
            rows = []
            for c in range(COLOURS):
                w = where_ref[c, s]
                mine = near[c][jnp.minimum(w, 7)]
                rows.append(jnp.where(w < 8, mine, late[c][jnp.maximum(w - 8, 0)]))
            hi, lo = split(jnp.concatenate(rows, axis=0))
            at = slice(s * SUB, (s + 1) * SUB)
            ah[at, :] = hi
            al[at, :] = lo

    dot = functools.partial(jnp.dot, preferred_element_type=f32)
    acc = dot(ah[...], bh_ref[0]) + dot(ah[...], bl_ref[0]) + dot(al[...], bh_ref[0])
    for i in range(NZ):
        for t in range(NB // TILE):
            o_ref[i, t] = acc[2 * SUB * i : 2 * SUB * (i + 1), t * TILE : (t + 1) * TILE]


def multiply(held, bh, bl, where):
    blocks, depth, _ = bh.shape
    m = NZ * 2 * SUB
    chunk = pl.BlockSpec((1, depth, NB), lambda n: (n, 0, 0))
    return call(
        mm_kernel,
        jax.ShapeDtypeStruct((NZ, blocks * NB // TILE, 2 * SUB, TILE), f32),
        grid=(blocks,),
        in_specs=[pl.BlockSpec(memory_space=pltpu.SMEM)]
        + [pl.BlockSpec(h.shape, lambda n: (0, 0, 0)) for h in held]
        + [chunk, chunk],
        out_specs=pl.BlockSpec((NZ, NB // TILE, 2 * SUB, TILE), lambda n: (0, n, 0, 0)),
        scratch_shapes=[pltpu.VMEM((m, depth), bf16), pltpu.VMEM((m, depth), bf16)],
        vmem=32,
        flops=6 * m * depth * blocks * NB,
        nbytes=4 * depth * blocks * NB,
    )(where, *held, bh, bl)


def far_kernel(mine_ref, got_ref, p_ref, m_ref):
    half = TPD // 2
    p_ref[...] = mine_ref[0, :half] + got_ref[0, :half]
    m_ref[...] = mine_ref[0, half:] + got_ref[0, half:]


def far(mine, got):
    block = (1,) + mine.shape[1:]
    shape = jax.ShapeDtypeStruct((TPD // 2,) + mine.shape[2:], f32)
    spec = pl.BlockSpec(block, lambda n: (0, 0, 0, 0))
    whole = pl.BlockSpec(shape.shape, lambda n: (0, 0, 0))
    return call(far_kernel, (shape, shape), grid=(1,), in_specs=[spec, spec], out_specs=(whole, whole), nbytes=3 * 1024 * 512)(mine, got)


def near_kernel(mine_ref, got_ref, gp_ref, gm_ref, p_ref, m_ref):
    half = TPD // 2
    p_ref[:half] = mine_ref[0, :half] + got_ref[0, :half] + gp_ref[...]
    p_ref[half:] = mine_ref[0, half:] + got_ref[0, half:]
    m_ref[:half] = mine_ref[1, :half] + got_ref[1, :half]
    m_ref[half:] = mine_ref[1, half:] + got_ref[1, half:] + gm_ref[...]


def near(mine, got, gp, gm):
    rows = mine.shape[2]
    two = pl.BlockSpec((pl.Element(2), pl.Element(TPD), pl.Element(rows), pl.Element(TILE)), lambda n: (1, 0, 0, 0))
    part = pl.BlockSpec(gp.shape, lambda n: (0, 0, 0))
    shape = jax.ShapeDtypeStruct(mine.shape[1:], f32)
    whole = pl.BlockSpec(shape.shape, lambda n: (0, 0, 0))
    return call(near_kernel, (shape, shape), grid=(1,), in_specs=[two, two, part, part], out_specs=(whole, whole), nbytes=7 * 1024 * 512)(mine, got, gp, gm)


def gather_kernel(idx_ref, *refs):
    ins, (out_ref, scr) = refs[:-2], refs[-2:]
    base = 0
    for c in range(PARTS):
        mine, got, rp, rm = ins[4 * c : 4 * c + 4]
        rows = 2 * SUB
        for t in range(TPD):
            scr[base + t * rows : base + (t + 1) * rows, :] = mine[0, t] + got[0, t] + rp[t] + rm[t]
        base += TPD * rows

    def step(g, carry):
        for k in range(16):
            i = g * 16 + k
            out_ref[pl.ds(i, 1), :] = scr[pl.ds(idx_ref[i], 1), :]
        return carry

    lax.fori_loop(0, ROWS * TPD // 16, step, 0)


def gather(idx, parts):
    units = ROWS * TPD
    specs = [pl.BlockSpec(memory_space=pltpu.SMEM)]
    flat = []
    for mine, got, rp, rm in parts:
        own = pl.BlockSpec((1,) + mine.shape[1:], lambda n: (NZ - 1, 0, 0, 0))
        whole = pl.BlockSpec(rp.shape, lambda n: (0, 0, 0))
        specs += [own, own, whole, whole]
        flat += [mine, got, rp, rm]
    return call(
        gather_kernel,
        jax.ShapeDtypeStruct((units, TILE), f32),
        grid=(1,),
        in_specs=specs,
        out_specs=pl.BlockSpec((units, TILE), lambda n: (0, 0)),
        scratch_shapes=[pltpu.VMEM((units, TILE), f32)],
        nbytes=5 * units * TILE * 4,
    )(idx, *flat)


def finish_kernel(place_ref, got_ref, den_ref, ch_ref, cl_ref, up_ref, ct_ref, scr):
    def step(g, carry):
        for k in range(16):
            i = g * 16 + k
            scr[pl.ds(place_ref[i], 1), :] = got_ref[pl.ds(i, 1), :]
        return carry

    lax.fori_loop(0, ROWS * TPD // 16, step, 0)
    for t in range(TPD):
        at = slice(t * TILE, (t + 1) * TILE)
        up_ref[:, at] = scr[at, :] / den_ref[:, at]
    dot = functools.partial(jnp.dot, preferred_element_type=f32)
    for k in range(TPD * TILE // RB):
        at = slice(k * RB, (k + 1) * RB)
        hi, lo = split(up_ref[:, at])
        ct_ref[:, at] = dot(hi, ch_ref[at, :]) + dot(hi, cl_ref[at, :]) + dot(lo, ch_ref[at, :])


def finish(place, got, den, ch, cl):
    shape = jax.ShapeDtypeStruct(den.shape, f32)
    whole = lambda s: pl.BlockSpec(s, lambda n: (0, 0))
    return call(
        finish_kernel,
        (shape, shape),
        grid=(1,),
        in_specs=[pl.BlockSpec(memory_space=pltpu.SMEM), whole(got.shape), whole(den.shape), whole(ch.shape), whole(cl.shape)],
        out_specs=(whole(den.shape), whole(den.shape)),
        scratch_shapes=[pltpu.VMEM(got.shape, f32)],
        nbytes=8 << 20,
    )(place, got, den, ch, cl)


def plan(destination):
    flat = destination.reshape(-1)
    out_row = flat // VT
    out_tile = flat % VT
    owner = out_row // ROWS * (VT // TPD) + out_tile // TPD
    place = out_tile % TPD * ROWS + out_row % ROWS
    unit = jnp.arange(ROWS * TPD, dtype=jnp.int32)
    row, tile = unit // TPD, unit % TPD
    block, colour, part, sub = row // 64, row // 16 % COLOURS, row // 8 % PARTS, row % 8
    at = part * (TPD * 2 * SUB) + tile * (2 * SUB) + block * SUB + colour * 8 + sub
    key = lax.sort((owner << 22) | (at << 11) | place)
    return (key >> 11) & 2047, key & 2047


def ring(step):
    return [(i, (i + step) % NZ) for i in range(NZ)]


EVEN = [(i, i ^ 1) for i in range(4)]
ODD = [(i, i ^ 3) for i in range(4)]
EXCHANGES = {"xe": ("x", EVEN), "xo": ("x", ODD), "ye": ("y", EVEN), "yo": ("y", ODD)}
ORDERS = [["xe", "xo", "ye", "yo"], ["xo", "ye", "yo", "xe"], ["ye", "yo", "xe", "xo"], ["yo", "xe", "xo", "ye"]]


def exchange(value, name):
    axis, pairs = EXCHANGES[name]
    return lax.ppermute(value, axis, pairs)


def places(ys, xs):
    dx = lax.axis_index("x") ^ xs
    dy = lax.axis_index("y") ^ ys
    bits = {"xe": (dx & 1) ^ (dx >> 1), "xo": dx >> 1, "ye": (dy & 1) ^ (dy >> 1), "yo": dy >> 1}
    return jnp.stack([sum(bits[name] << k for k, name in enumerate(order)) for order in ORDERS])


def after(value, *others):
    return lax.optimization_barrier((value,) + others)[0]


def body(amplitudes, integrals, integral_mask, denominators, cycle_tiles, cycle_mask, destination):
    everyone = ("z", "core", "y", "x")
    z = lax.axis_index("z")
    core = lax.axis_index("core")
    depth = integrals.shape[0]

    towards = jnp.repeat(jnp.array([2, 1, 3, 0], jnp.int32), 2)
    shard = jnp.array([0, 1] * NZ, jnp.int32)
    ys = (z + towards) % NZ
    own = places(ys, 2 * core + shard)
    other = places(ys, 2 * (1 - core) + shard)

    rows = amplitudes.reshape(COLOURS, PARTS, 1, 8, depth)
    bufs = [rows[c] for c in range(COLOURS)]
    got = [exchange(bufs[c], ORDERS[c][0]) for c in range(COLOURS)]
    bufs = [jnp.concatenate([b, g], axis=1) for b, g in zip(bufs, got)]
    got = [exchange(bufs[c], ORDERS[c][1]) for c in range(COLOURS)]
    halves = [[jnp.concatenate([b[p], g[p]], axis=0) for b, g in zip(bufs, got)] for p in range(PARTS)]

    half = integrals.shape[1] // NB // 2
    b_first = prepare_integrals(integrals, integral_mask, 0, half)
    bh, bl = prepare_integrals(integrals, integral_mask, half, half, b_first)

    parts = []
    last = None
    for p in range(PARTS):
        bufs = halves[p]
        if last is not None:
            bufs = list(lax.optimization_barrier(tuple(bufs) + tuple(last)))[:COLOURS]
        got = [exchange(bufs[c], ORDERS[c][2]) for c in range(COLOURS)]
        last = got
        bufs = [jnp.concatenate([b, g], axis=0) for b, g in zip(bufs, got)]
        late = [exchange(bufs[c], ORDERS[c][3]) for c in range(COLOURS)]
        theirs = multiply(bufs + late, bh, bl, other)
        from_core = lax.ppermute(theirs, "core", [(0, 1), (1, 0)])
        mine = multiply(bufs + late, bh, bl, own)
        far_p, far_m = far(mine, from_core)
        gp = lax.ppermute(far_p, "z", ring(1))
        gm = lax.ppermute(far_m, "z", ring(-1))
        near_p, near_m = near(mine, from_core, gp, gm)
        rp = lax.ppermute(near_p, "z", ring(1))
        rm = lax.ppermute(near_m, "z", ring(-1))
        parts.append((mine, from_core, rp, rm))

    source, place = plan(after(destination, theirs))
    place = place.astype(f32).reshape(128, 1, CAP)
    got_place = lax.all_to_all(place, everyone, split_axis=0, concat_axis=0, tiled=True)
    got_place = got_place.reshape(-1).astype(jnp.int32)
    ch, cl = prepare_cycle(after(cycle_tiles, theirs), cycle_mask)

    sending = gather(after(source, got_place, ch, cl), parts).reshape(128, CAP, TILE)
    units = lax.all_to_all(sending, everyone, split_axis=0, concat_axis=0, tiled=True)
    return finish(got_place, units.reshape(-1, TILE), denominators, ch, cl)


def solution(mesh):
    row, col = ("z", "core"), ("y", "x")
    split_mesh = Mesh(mesh.devices.reshape(4, 2, 4, 4), row + col)
    return jax.shard_map(
        body,
        mesh=split_mesh,
        in_specs=(P(col, row), P(row, col), P(row, col), P(row, col), P(col, None), P(col, None), P(row, col)),
        out_specs=(P(row, col), P(row, col)),
        check_vma=False,
    )
```

```python
import functools

import jax
import jax.numpy as jnp
from jax import lax
from jax.experimental import pallas as pl
from jax.experimental.pallas import tpu as pltpu
from jax.sharding import Mesh, PartitionSpec as P

TILE = 128
RB = 512
VT = 256
ROWS = 128
TPD = 16
CAP = 16
NZ = 4
PARTS = 2
SUB = 32
COLOURS = 4
NB = 256
SLOTS = 4
MIB = 1 << 20

f32 = jnp.float32
bf16 = jnp.bfloat16


def split(x):
    hi = x.astype(bf16)
    return hi, (x - hi.astype(f32)).astype(bf16)


def call(kernel, out_shape, *, vmem=16, flops=0, nbytes=0, **kw):
    return pl.pallas_call(
        kernel,
        out_shape=out_shape,
        compiler_params=pltpu.CompilerParams(vmem_limit_bytes=vmem * MIB),
        cost_estimate=pl.CostEstimate(flops=flops, bytes_accessed=nbytes, transcendentals=0),
        **kw,
    )


def masked_split(mask_ref, x_ref, mi, mj, i, j):
    m = mask_ref[mi, mj].astype(f32)
    return split(x_ref[i * TILE : (i + 1) * TILE, j * TILE : (j + 1) * TILE] * m)


def cycle_kernel(mask_ref, x_ref, hi_ref, lo_ref):
    for i in range(RB // TILE):
        for j in range(RB // TILE):
            hi, lo = masked_split(mask_ref, x_ref, pl.program_id(0) * (RB // TILE) + i, j, i, j)
            at = (slice(i * TILE, (i + 1) * TILE), slice(j * TILE, (j + 1) * TILE))
            hi_ref[at] = hi
            lo_ref[at] = lo


def prepare_cycle(x, mask):
    spec = pl.BlockSpec((RB, RB), lambda n: (n, 0))
    out = jax.ShapeDtypeStruct(x.shape, bf16)
    return call(
        cycle_kernel,
        (out, out),
        grid=(x.shape[0] // RB,),
        in_specs=[pl.BlockSpec(memory_space=pltpu.SMEM), spec],
        out_specs=(spec, spec),
        nbytes=x.size * 8,
        flops=x.size * 4,
    )(mask, x)


def mm_kernel(where_ref, mask_ref, *refs):
    held, b_ref, o_ref, ah, al, slots, sems = refs[:-6], *refs[-6:]
    near, late = held[:COLOURS], held[COLOURS:]
    blocks = b_ref.shape[1] // NB
    per = NB // TILE

    def fetch(n):
        slot = n % SLOTS
        at = pl.ds(pl.multiple_of(n * NB, NB), NB)
        return pltpu.make_async_copy(b_ref.at[:, at], slots.at[slot], sems.at[slot])

    for n in range(SLOTS):
        fetch(n).start()

    for s in range(2 * NZ):
        rows = []
        for c in range(COLOURS):
            w = where_ref[c, s]
            mine = near[c][jnp.minimum(w, 7)]
            rows.append(jnp.where(w < 8, mine, late[c][jnp.maximum(w - 8, 0)]))
        hi, lo = split(jnp.concatenate(rows, axis=0))
        at = slice(s * SUB, (s + 1) * SUB)
        ah[at, :] = hi
        al[at, :] = lo

    dot = functools.partial(jnp.dot, preferred_element_type=f32)
    tiles = range(b_ref.shape[0] // TILE)

    def step(n, carry):
        fetch(n).wait()
        x = slots.at[n % SLOTS]
        terms = [[masked_split(mask_ref, x, i, n * per + j, i, j) for j in range(per)] for i in tiles]
        bh, bl = (jnp.concatenate([jnp.concatenate([t[k] for t in row], axis=1) for row in terms], axis=0) for k in range(2))
        acc = dot(ah[...], bh) + dot(ah[...], bl) + dot(al[...], bh)
        for i in range(NZ):
            for t in range(per):
                o_ref[i, n * per + t] = acc[2 * SUB * i : 2 * SUB * (i + 1), t * TILE : (t + 1) * TILE]

        @pl.when(n + SLOTS < blocks)
        def _():
            fetch(n + SLOTS).start()

        return carry

    lax.fori_loop(0, blocks, step, 0)


def multiply(held, integrals, mask, where):
    depth, cols = integrals.shape
    m = NZ * 2 * SUB
    smem = pl.BlockSpec(memory_space=pltpu.SMEM)
    vmem = pl.BlockSpec(memory_space=pltpu.VMEM)
    return call(
        mm_kernel,
        jax.ShapeDtypeStruct((NZ, cols // TILE, 2 * SUB, TILE), f32),
        in_specs=[smem, smem] + [vmem] * len(held) + [pl.BlockSpec(memory_space=pltpu.HBM)],
        out_specs=vmem,
        scratch_shapes=[
            pltpu.VMEM((m, depth), bf16),
            pltpu.VMEM((m, depth), bf16),
            pltpu.VMEM((SLOTS, depth, NB), f32),
            pltpu.SemaphoreType.DMA((SLOTS,)),
        ],
        vmem=48,
        flops=6 * m * depth * cols,
        nbytes=4 * depth * cols,
    )(where, mask, *held, integrals)


def far_kernel(mine_ref, got_ref, p_ref, m_ref):
    half = TPD // 2
    p_ref[...] = mine_ref[0, :half] + got_ref[0, :half]
    m_ref[...] = mine_ref[0, half:] + got_ref[0, half:]


def far(mine, got):
    block = (1,) + mine.shape[1:]
    shape = jax.ShapeDtypeStruct((TPD // 2,) + mine.shape[2:], f32)
    spec = pl.BlockSpec(block, lambda n: (0, 0, 0, 0))
    whole = pl.BlockSpec(shape.shape, lambda n: (0, 0, 0))
    return call(far_kernel, (shape, shape), grid=(1,), in_specs=[spec, spec], out_specs=(whole, whole), nbytes=3 * 1024 * 512)(mine, got)


def near_kernel(mine_ref, got_ref, gp_ref, gm_ref, p_ref, m_ref):
    half = TPD // 2
    p_ref[:half] = mine_ref[0, :half] + got_ref[0, :half] + gp_ref[...]
    p_ref[half:] = mine_ref[0, half:] + got_ref[0, half:]
    m_ref[:half] = mine_ref[1, :half] + got_ref[1, :half]
    m_ref[half:] = mine_ref[1, half:] + got_ref[1, half:] + gm_ref[...]


def near(mine, got, gp, gm):
    rows = mine.shape[2]
    two = pl.BlockSpec((pl.Element(2), pl.Element(TPD), pl.Element(rows), pl.Element(TILE)), lambda n: (1, 0, 0, 0))
    part = pl.BlockSpec(gp.shape, lambda n: (0, 0, 0))
    shape = jax.ShapeDtypeStruct(mine.shape[1:], f32)
    whole = pl.BlockSpec(shape.shape, lambda n: (0, 0, 0))
    return call(near_kernel, (shape, shape), grid=(1,), in_specs=[two, two, part, part], out_specs=(whole, whole), nbytes=7 * 1024 * 512)(mine, got, gp, gm)


def gather_kernel(idx_ref, *refs):
    ins, (out_ref, scr) = refs[:-2], refs[-2:]
    base = 0
    for c in range(PARTS):
        mine, got, rp, rm = ins[4 * c : 4 * c + 4]
        rows = 2 * SUB
        for t in range(TPD):
            scr[base + t * rows : base + (t + 1) * rows, :] = mine[0, t] + got[0, t] + rp[t] + rm[t]
        base += TPD * rows

    def step(g, carry):
        for k in range(16):
            i = g * 16 + k
            out_ref[pl.ds(i, 1), :] = scr[pl.ds(idx_ref[i], 1), :]
        return carry

    lax.fori_loop(0, ROWS * TPD // 16, step, 0)


def gather(idx, parts):
    units = ROWS * TPD
    specs = [pl.BlockSpec(memory_space=pltpu.SMEM)]
    flat = []
    for mine, got, rp, rm in parts:
        own = pl.BlockSpec((1,) + mine.shape[1:], lambda n: (NZ - 1, 0, 0, 0))
        whole = pl.BlockSpec(rp.shape, lambda n: (0, 0, 0))
        specs += [own, own, whole, whole]
        flat += [mine, got, rp, rm]
    return call(
        gather_kernel,
        jax.ShapeDtypeStruct((units, TILE), f32),
        grid=(1,),
        in_specs=specs,
        out_specs=pl.BlockSpec((units, TILE), lambda n: (0, 0)),
        scratch_shapes=[pltpu.VMEM((units, TILE), f32)],
        nbytes=5 * units * TILE * 4,
    )(idx, *flat)


def finish_kernel(place_ref, got_ref, den_ref, ch_ref, cl_ref, up_ref, ct_ref, scr):
    def step(g, carry):
        for k in range(16):
            i = g * 16 + k
            scr[pl.ds(place_ref[i], 1), :] = got_ref[pl.ds(i, 1), :]
        return carry

    lax.fori_loop(0, ROWS * TPD // 16, step, 0)
    for t in range(TPD):
        at = slice(t * TILE, (t + 1) * TILE)
        up_ref[:, at] = scr[at, :] / den_ref[:, at]
    dot = functools.partial(jnp.dot, preferred_element_type=f32)
    for k in range(TPD * TILE // RB):
        at = slice(k * RB, (k + 1) * RB)
        hi, lo = split(up_ref[:, at])
        ct_ref[:, at] = dot(hi, ch_ref[at, :]) + dot(hi, cl_ref[at, :]) + dot(lo, ch_ref[at, :])


def finish(place, got, den, ch, cl):
    shape = jax.ShapeDtypeStruct(den.shape, f32)
    whole = lambda s: pl.BlockSpec(s, lambda n: (0, 0))
    return call(
        finish_kernel,
        (shape, shape),
        grid=(1,),
        in_specs=[pl.BlockSpec(memory_space=pltpu.SMEM), whole(got.shape), whole(den.shape), whole(ch.shape), whole(cl.shape)],
        out_specs=(whole(den.shape), whole(den.shape)),
        scratch_shapes=[pltpu.VMEM(got.shape, f32)],
        nbytes=8 << 20,
    )(place, got, den, ch, cl)


def plan(destination):
    flat = destination.reshape(-1)
    out_row = flat // VT
    out_tile = flat % VT
    owner = out_row // ROWS * (VT // TPD) + out_tile // TPD
    place = out_tile % TPD * ROWS + out_row % ROWS
    unit = jnp.arange(ROWS * TPD, dtype=jnp.int32)
    row, tile = unit // TPD, unit % TPD
    block, colour, part, sub = row // 64, row // 16 % COLOURS, row // 8 % PARTS, row % 8
    at = part * (TPD * 2 * SUB) + tile * (2 * SUB) + block * SUB + colour * 8 + sub
    key = lax.sort((owner << 22) | (at << 11) | place)
    return (key >> 11) & 2047, key & 2047


def ring(step):
    return [(i, (i + step) % NZ) for i in range(NZ)]


EVEN = [(i, i ^ 1) for i in range(4)]
ODD = [(i, i ^ 3) for i in range(4)]
EXCHANGES = {"xe": ("x", EVEN), "xo": ("x", ODD), "ye": ("y", EVEN), "yo": ("y", ODD)}
ORDERS = [["xe", "xo", "ye", "yo"], ["xo", "ye", "yo", "xe"], ["ye", "yo", "xe", "xo"], ["yo", "xe", "xo", "ye"]]


def exchange(value, name):
    axis, pairs = EXCHANGES[name]
    return lax.ppermute(value, axis, pairs)


def places(ys, xs):
    dx = lax.axis_index("x") ^ xs
    dy = lax.axis_index("y") ^ ys
    bits = {"xe": (dx & 1) ^ (dx >> 1), "xo": dx >> 1, "ye": (dy & 1) ^ (dy >> 1), "yo": dy >> 1}
    return jnp.stack([sum(bits[name] << k for k, name in enumerate(order)) for order in ORDERS])


def after(value, *others):
    return lax.optimization_barrier((value,) + others)[0]


def body(amplitudes, integrals, integral_mask, denominators, cycle_tiles, cycle_mask, destination):
    everyone = ("z", "core", "y", "x")
    z = lax.axis_index("z")
    core = lax.axis_index("core")
    depth = integrals.shape[0]

    towards = jnp.repeat(jnp.array([2, 1, 3, 0], jnp.int32), 2)
    shard = jnp.array([0, 1] * NZ, jnp.int32)
    ys = (z + towards) % NZ
    own = places(ys, 2 * core + shard)
    other = places(ys, 2 * (1 - core) + shard)

    rows = amplitudes.reshape(COLOURS, PARTS, 1, 8, depth)
    bufs = [rows[c] for c in range(COLOURS)]
    got = [exchange(bufs[c], ORDERS[c][0]) for c in range(COLOURS)]
    source, place = plan(destination)
    bufs = [jnp.concatenate([b, g], axis=1) for b, g in zip(bufs, got)]
    bufs[-1] = after(bufs[-1], source)
    got = [exchange(bufs[c], ORDERS[c][1]) for c in range(COLOURS)]
    halves = [[jnp.concatenate([b[p], g[p]], axis=0) for b, g in zip(bufs, got)] for p in range(PARTS)]

    def third(bufs):
        got = [exchange(bufs[c], ORDERS[c][2]) for c in range(COLOURS)]
        return got, [jnp.concatenate([b, g], axis=0) for b, g in zip(bufs, got)]

    def fourth(bufs):
        return bufs + [exchange(bufs[c], ORDERS[c][3]) for c in range(COLOURS)]

    def product(held, where):
        return multiply(held, integrals, integral_mask, where)

    def swap(value):
        return lax.ppermute(value, "core", [(0, 1), (1, 0)])

    _, bufs = third(halves[0])
    held0 = fourth(bufs)
    ready = lax.optimization_barrier(tuple(halves[1]) + tuple(held0[COLOURS:]))
    got, bufs = third(list(ready[:COLOURS]))
    theirs0 = product(held0, other)
    from_core0 = swap(theirs0)
    held1 = fourth(bufs)
    mine0 = product(held0, after(own, *got))
    theirs1 = product(held1, after(other, mine0))
    from_core1 = swap(theirs1)
    mine1 = product(held1, own)

    ch, cl = prepare_cycle(after(cycle_tiles, theirs1), cycle_mask)
    sums = []
    for p, (mine, from_core) in enumerate([(mine0, from_core0), (mine1, from_core1)]):
        far_p, far_m = far(mine, from_core)
        gp = lax.ppermute(far_p, "z", ring(1))
        gm = lax.ppermute(far_m, "z", ring(-1))
        if p == PARTS - 1:
            gp = after(gp, ch, cl)
        near_p, near_m = near(mine, from_core, gp, gm)
        rp = lax.ppermute(near_p, "z", ring(1))
        rm = lax.ppermute(near_m, "z", ring(-1))
        sums.append((mine, from_core, rp, rm))

    place = after(place, theirs1).astype(f32).reshape(128, 1, CAP)
    got_place = lax.all_to_all(place, everyone, split_axis=0, concat_axis=0, tiled=True)
    got_place = got_place.reshape(-1).astype(jnp.int32)
    sending = gather(after(source, got_place, ch, cl), sums).reshape(128, CAP, TILE)
    units = lax.all_to_all(sending, everyone, split_axis=0, concat_axis=0, tiled=True)
    return finish(got_place, units.reshape(-1, TILE), denominators, ch, cl)


def solution(mesh):
    row, col = ("z", "core"), ("y", "x")
    split_mesh = Mesh(mesh.devices.reshape(4, 2, 4, 4), row + col)
    return jax.shard_map(
        body,
        mesh=split_mesh,
        in_specs=(P(col, row), P(row, col), P(row, col), P(row, col), P(col, None), P(col, None), P(row, col)),
        out_specs=(P(row, col), P(row, col)),
        check_vma=False,
    )
```

```python
import functools

import jax
import jax.numpy as jnp
from jax import lax
from jax.experimental import pallas as pl
from jax.experimental.pallas import tpu as pltpu
from jax.sharding import Mesh, PartitionSpec as P

TILE = 128
RB = 512
VT = 256
ROWS = 128
TPD = 16
CAP = 16
NZ = 4
PARTS = 2
PART = TPD // PARTS
COLOURS = 4
NB = 256
SLOTS = 3
MIB = 1 << 20

f32 = jnp.float32
bf16 = jnp.bfloat16


def split(x):
    hi = x.astype(bf16)
    return hi, (x - hi.astype(f32)).astype(bf16)


def call(kernel, out_shape, *, vmem=16, flops=0, nbytes=0, **kw):
    return pl.pallas_call(
        kernel,
        out_shape=out_shape,
        compiler_params=pltpu.CompilerParams(vmem_limit_bytes=vmem * MIB),
        cost_estimate=pl.CostEstimate(flops=flops, bytes_accessed=nbytes, transcendentals=0),
        **kw,
    )


def masked_split(mask_ref, x_ref, mi, mj, i, j):
    m = mask_ref[mi, mj].astype(f32)
    return split(x_ref[i * TILE : (i + 1) * TILE, j * TILE : (j + 1) * TILE] * m)


def cycle_kernel(mask_ref, x_ref, hi_ref, lo_ref):
    for i in range(RB // TILE):
        for j in range(RB // TILE):
            hi, lo = masked_split(mask_ref, x_ref, pl.program_id(0) * (RB // TILE) + i, j, i, j)
            at = (slice(i * TILE, (i + 1) * TILE), slice(j * TILE, (j + 1) * TILE))
            hi_ref[at] = hi
            lo_ref[at] = lo


def prepare_cycle(x, mask):
    spec = pl.BlockSpec((RB, RB), lambda n: (n, 0))
    out = jax.ShapeDtypeStruct(x.shape, bf16)
    return call(
        cycle_kernel,
        (out, out),
        grid=(x.shape[0] // RB,),
        in_specs=[pl.BlockSpec(memory_space=pltpu.SMEM), spec],
        out_specs=(spec, spec),
        nbytes=x.size * 8,
        flops=x.size * 4,
    )(mask, x)


def mm_body(first, mask_ref, ah, al, b_ref, o_ref, slots, sems, before):
    per = NB // TILE
    blocks = PART // per

    def fetch(n):
        slot = n % SLOTS
        at = pl.ds(pl.multiple_of((first + n) * NB, NB), NB)
        return pltpu.make_async_copy(b_ref.at[:, at], slots.at[slot], sems.at[slot])

    for n in range(SLOTS):
        fetch(n).start()
    before()
    dot = functools.partial(jnp.dot, preferred_element_type=f32)
    tiles = range(b_ref.shape[0] // TILE)

    def step(n, carry):
        fetch(n).wait()
        x = slots.at[n % SLOTS]
        terms = [[masked_split(mask_ref, x, i, (first + n) * per + j, i, j) for j in range(per)] for i in tiles]
        bh, bl = (jnp.concatenate([jnp.concatenate([t[k] for t in row], axis=1) for row in terms], axis=0) for k in range(2))
        acc = dot(ah[...], bh) + dot(ah[...], bl) + dot(al[...], bh)
        for i in range(NZ):
            for t in range(per):
                o_ref[i, n * per + t] = acc[ROWS * i : ROWS * (i + 1), t * TILE : (t + 1) * TILE]

        @pl.when(n + SLOTS < blocks)
        def _():
            fetch(n + SLOTS).start()

        return carry

    lax.fori_loop(0, blocks, step, 0)


def mm_first_kernel(where_ref, mask_ref, *refs):
    held, b_ref, o_ref, ah, al, slots, sems = refs[:-6], *refs[-6:]
    near, late = held[:COLOURS], held[COLOURS:]
    rows = ROWS // 2 // COLOURS

    def gather_rows():
        for s in range(2 * NZ):
            for c in range(COLOURS):
                w = where_ref[c, s]
                mine = near[c][jnp.minimum(w, 7)]
                hi, lo = split(jnp.where(w < 8, mine, late[c][jnp.maximum(w - 8, 0)]))
                at = slice((s * COLOURS + c) * rows, (s * COLOURS + c + 1) * rows)
                ah[at, :] = hi
                al[at, :] = lo

    mm_body(0, mask_ref, ah, al, b_ref, o_ref, slots, sems, gather_rows)


def mm_next_kernel(mask_ref, ah, al, b_ref, o_ref, slots, sems, *, first):
    mm_body(first, mask_ref, ah, al, b_ref, o_ref, slots, sems, lambda: None)


SMEM = pl.BlockSpec(memory_space=pltpu.SMEM)
VMEM = pl.BlockSpec(memory_space=pltpu.VMEM)


def multiply(kernel, inputs, integrals, keep):
    depth, _ = integrals.shape
    m = NZ * ROWS
    shapes = [jax.ShapeDtypeStruct((NZ, PART, ROWS, TILE), f32)]
    shapes += [jax.ShapeDtypeStruct((m, depth), bf16)] * (2 if keep else 0)
    return call(
        kernel,
        tuple(shapes),
        in_specs=[SMEM if x.dtype == jnp.int32 else VMEM for x in inputs] + [pl.BlockSpec(memory_space=pltpu.HBM)],
        out_specs=(VMEM,) * len(shapes),
        scratch_shapes=[pltpu.VMEM((SLOTS, depth, NB), f32), pltpu.SemaphoreType.DMA((SLOTS,))],
        vmem=40,
        flops=40 * 6 * m * depth * PART * TILE,
        nbytes=4 * depth * PART * TILE,
    )(*inputs, integrals)


def far_kernel(mine_ref, got_ref, p_ref, m_ref, plus_ref, minus_ref, own_ref):
    half = PART // 2
    p_ref[...] = mine_ref[0, :half] + got_ref[0, :half]
    m_ref[...] = mine_ref[0, half:] + got_ref[0, half:]
    plus_ref[...] = mine_ref[1] + got_ref[1]
    minus_ref[...] = mine_ref[2] + got_ref[2]
    own_ref[...] = mine_ref[3] + got_ref[3]


def small(kernel, inputs, shapes, scratch=()):
    shapes = tuple(jax.ShapeDtypeStruct(s, f32) for s in shapes)
    return call(
        kernel,
        shapes,
        in_specs=[SMEM if x.dtype == jnp.int32 else VMEM for x in inputs],
        out_specs=(VMEM,) * len(shapes),
        scratch_shapes=[pltpu.VMEM(s, f32) for s in scratch],
        nbytes=4 * sum(x.size for x in inputs),
    )(*inputs)


def far(mine, got):
    part = (PART, ROWS, TILE)
    half = (PART // 2, ROWS, TILE)
    return small(far_kernel, (mine, got), (half, half, part, part, part))


def near_kernel(plus_ref, minus_ref, gp_ref, gm_ref, p_ref, m_ref):
    half = PART // 2
    p_ref[:half] = plus_ref[:half] + gp_ref[...]
    p_ref[half:] = plus_ref[half:]
    m_ref[:half] = minus_ref[:half]
    m_ref[half:] = minus_ref[half:] + gm_ref[...]


def near(plus, minus, gp, gm):
    return small(near_kernel, (plus, minus, gp, gm), (plus.shape, plus.shape))


def gather_kernel(idx_ref, *refs):
    ins, (out_ref, scr) = refs[:-2], refs[-2:]
    for p in range(PARTS):
        own, rp, rm = ins[3 * p : 3 * p + 3]
        for t in range(PART):
            at = (p * PART + t) * ROWS
            scr[at : at + ROWS, :] = own[t] + rp[t] + rm[t]

    def step(g, carry):
        for k in range(CAP):
            out_ref[pl.ds(g * CAP + k, 1), :] = scr[pl.ds(idx_ref[g * CAP + k], 1), :]
        return carry

    lax.fori_loop(0, ROWS * TPD // CAP, step, 0)


def gather(idx, parts):
    units = ROWS * TPD
    flat = [x for part in parts for x in part]
    return small(gather_kernel, (idx, *flat), ((units, TILE),), ((units, TILE),))[0]


def finish_kernel(place_ref, got_ref, den_ref, ch_ref, cl_ref, up_ref, ct_ref, scr):
    def step(g, carry):
        for k in range(CAP):
            scr[pl.ds(place_ref[g * CAP + k], 1), :] = got_ref[pl.ds(g * CAP + k, 1), :]
        return carry

    lax.fori_loop(0, ROWS * TPD // CAP, step, 0)
    for t in range(TPD):
        at = slice(t * TILE, (t + 1) * TILE)
        up_ref[:, at] = scr[at, :] / den_ref[:, at]
    dot = functools.partial(jnp.dot, preferred_element_type=f32)
    for k in range(TPD * TILE // RB):
        at = slice(k * RB, (k + 1) * RB)
        hi, lo = split(up_ref[:, at])
        ct_ref[:, at] = dot(hi, ch_ref[at, :]) + dot(hi, cl_ref[at, :]) + dot(lo, ch_ref[at, :])


def finish(place, got, den, ch, cl):
    shape = jax.ShapeDtypeStruct(den.shape, f32)
    whole = lambda s: pl.BlockSpec(s, lambda n: (0, 0))
    return call(
        finish_kernel,
        (shape, shape),
        grid=(1,),
        in_specs=[pl.BlockSpec(memory_space=pltpu.SMEM), whole(got.shape), whole(den.shape), whole(ch.shape), whole(cl.shape)],
        out_specs=(whole(den.shape), whole(den.shape)),
        scratch_shapes=[pltpu.VMEM((ROWS * TPD, TILE), f32)],
        nbytes=8 << 20,
    )(place, got, den, ch, cl)


def plan(destination):
    flat = destination.reshape(-1)
    out_row = flat // VT
    out_tile = flat % VT
    owner = out_row // ROWS * (VT // TPD) + out_tile // TPD
    place = out_tile % TPD * ROWS + out_row % ROWS
    unit = jnp.arange(ROWS * TPD, dtype=jnp.int32)
    row, tile = unit // TPD, unit % TPD
    at = tile * ROWS + row
    key = lax.sort((owner << 22) | (at << 11) | place)
    return (key >> 11) & 2047, key & 2047


def ring(step):
    return [(i, (i + step) % NZ) for i in range(NZ)]


EVEN = [(i, i ^ 1) for i in range(4)]
ODD = [(i, i ^ 3) for i in range(4)]
EXCHANGES = {"xe": ("x", EVEN), "xo": ("x", ODD), "ye": ("y", EVEN), "yo": ("y", ODD)}
ORDERS = [["xe", "xo", "ye", "yo"], ["xo", "ye", "yo", "xe"], ["ye", "yo", "xe", "xo"], ["yo", "xe", "xo", "ye"]]


def exchange(value, name):
    axis, pairs = EXCHANGES[name]
    return lax.ppermute(value, axis, pairs)


def places(ys, xs):
    dx = lax.axis_index("x") ^ xs
    dy = lax.axis_index("y") ^ ys
    bits = {"xe": (dx & 1) ^ (dx >> 1), "xo": dx >> 1, "ye": (dy & 1) ^ (dy >> 1), "yo": dy >> 1}
    return jnp.stack([sum(bits[name] << k for k, name in enumerate(order)) for order in ORDERS])


def after(value, *others):
    return lax.optimization_barrier((value,) + others)[0]


def body(amplitudes, integrals, integral_mask, denominators, cycle_tiles, cycle_mask, destination):
    everyone = ("z", "core", "y", "x")
    z = lax.axis_index("z")
    core = lax.axis_index("core")
    depth = integrals.shape[0]

    towards = jnp.repeat(jnp.array([2, 1, 3, 0], jnp.int32), 2)
    shard = jnp.array([0, 1] * NZ, jnp.int32)
    ys = (z + towards) % NZ
    own = places(ys, 2 * core + shard)
    other = places(ys, 2 * (1 - core) + shard)

    rows = amplitudes.reshape(COLOURS, 1, 64 // COLOURS, depth)
    bufs = [rows[c] for c in range(COLOURS)]

    def exchanged(k):
        got = [exchange(bufs[c], ORDERS[c][k]) for c in range(COLOURS)]
        return got, [jnp.concatenate([b, g], axis=0) for b, g in zip(bufs, got)]

    _, bufs = exchanged(0)
    got, bufs = exchanged(1)
    source, place = plan(after(destination, *got))
    _, bufs = exchanged(2)
    bufs[-1], source, place = lax.optimization_barrier((bufs[-1], source, place))
    late = [exchange(bufs[c], ORDERS[c][3]) for c in range(COLOURS)]
    held = (*bufs, *late)

    place = place.astype(f32).reshape(128, 1, CAP)
    got_place = lax.all_to_all(place, everyone, split_axis=0, concat_axis=0, tiled=True)
    got_place = got_place.reshape(-1).astype(jnp.int32)
    ch, cl = prepare_cycle(after(cycle_tiles, *bufs), cycle_mask)
    other, got_place, ch, cl, source = lax.optimization_barrier((other, got_place, ch, cl, source))

    def swap(value):
        return lax.ppermute(value, "core", [(0, 1), (1, 0)])

    def along_z(p, m):
        return lax.ppermute(p, "z", ring(1)), lax.ppermute(m, "z", ring(-1))

    def first_product(where):
        return multiply(mm_first_kernel, (where, integral_mask, *held), integrals, True)

    def next_product(mask, hi, lo):
        kernel = functools.partial(mm_next_kernel, first=PART * TILE // NB)
        return multiply(kernel, (mask, hi, lo), integrals, False)[0]

    theirs0, other_hi, other_lo = first_product(other)
    from_core0 = swap(theirs0)
    mine0, own_hi, own_lo = first_product(after(own, theirs0))
    p0, m0, plus0, minus0, base0 = far(mine0, from_core0)
    gp0, gm0 = along_z(p0, m0)
    theirs1 = next_product(after(integral_mask, base0), other_hi, other_lo)
    from_core1 = swap(theirs1)
    near0 = near(plus0, minus0, gp0, gm0)
    rp0, rm0 = along_z(*near0)
    mine1 = next_product(after(integral_mask, *near0), own_hi, own_lo)
    p1, m1, plus1, minus1, base1 = far(mine1, from_core1)
    gp1, gm1 = along_z(p1, m1)
    rp1, rm1 = along_z(*near(plus1, minus1, after(gp1, rp0, rm0), gm1))

    sending = gather(source, ((base0, rp0, rm0), (base1, rp1, rm1))).reshape(128, CAP, TILE)
    units = lax.all_to_all(sending, everyone, split_axis=0, concat_axis=0, tiled=True)
    return finish(got_place, units.reshape(-1, TILE), denominators, ch, cl)


def solution(mesh):
    row, col = ("z", "core"), ("y", "x")
    split_mesh = Mesh(mesh.devices.reshape(4, 2, 4, 4), row + col)
    return jax.shard_map(
        body,
        mesh=split_mesh,
        in_specs=(P(col, row), P(row, col), P(row, col), P(row, col), P(col, None), P(col, None), P(row, col)),
        out_specs=(P(row, col), P(row, col)),
        check_vma=False,
    )
```

```python
import functools

import jax
import jax.numpy as jnp
from jax import lax
from jax.experimental import pallas as pl
from jax.experimental.pallas import tpu as pltpu
from jax.sharding import Mesh, PartitionSpec as P

TILE = 128
RB = 512
VT = 256
ROWS = 128
TPD = 16
CAP = 16
NZ = 4
PARTS = (10, 6)
COLOURS = 4
NB = 256
SLOTS = 3
MIB = 1 << 20

f32 = jnp.float32
bf16 = jnp.bfloat16


def split(x):
    hi = x.astype(bf16)
    return hi, (x - hi.astype(f32)).astype(bf16)


def call(kernel, out_shape, *, vmem=16, flops=0, nbytes=0, **kw):
    return pl.pallas_call(
        kernel,
        out_shape=out_shape,
        compiler_params=pltpu.CompilerParams(vmem_limit_bytes=vmem * MIB),
        cost_estimate=pl.CostEstimate(flops=flops, bytes_accessed=nbytes, transcendentals=0),
        **kw,
    )


def masked_split(mask_ref, x_ref, mi, mj, i, j):
    m = mask_ref[mi, mj].astype(f32)
    return split(x_ref[i * TILE : (i + 1) * TILE, j * TILE : (j + 1) * TILE] * m)


def cycle_kernel(mask_ref, x_ref, hi_ref, lo_ref):
    for i in range(RB // TILE):
        for j in range(RB // TILE):
            hi, lo = masked_split(mask_ref, x_ref, pl.program_id(0) * (RB // TILE) + i, j, i, j)
            at = (slice(i * TILE, (i + 1) * TILE), slice(j * TILE, (j + 1) * TILE))
            hi_ref[at] = hi
            lo_ref[at] = lo


def prepare_cycle(x, mask):
    spec = pl.BlockSpec((RB, RB), lambda n: (n, 0))
    out = jax.ShapeDtypeStruct(x.shape, bf16)
    return call(
        cycle_kernel,
        (out, out),
        grid=(x.shape[0] // RB,),
        in_specs=[pl.BlockSpec(memory_space=pltpu.SMEM), spec],
        out_specs=(spec, spec),
        nbytes=x.size * 8,
        flops=x.size * 4,
    )(mask, x)


def mm_body(first, tiles_out, mask_ref, ah, al, b_ref, o_ref, slots, sems, before):
    per = NB // TILE
    blocks = tiles_out // per

    def fetch(n):
        slot = n % SLOTS
        at = pl.ds(pl.multiple_of((first + n) * NB, NB), NB)
        return pltpu.make_async_copy(b_ref.at[:, at], slots.at[slot], sems.at[slot])

    for n in range(SLOTS):
        fetch(n).start()
    before()
    dot = functools.partial(jnp.dot, preferred_element_type=f32)
    tiles = range(b_ref.shape[0] // TILE)

    def step(n, carry):
        fetch(n).wait()
        x = slots.at[n % SLOTS]
        terms = [[masked_split(mask_ref, x, i, (first + n) * per + j, i, j) for j in range(per)] for i in tiles]
        bh, bl = (jnp.concatenate([jnp.concatenate([t[k] for t in row], axis=1) for row in terms], axis=0) for k in range(2))
        acc = dot(ah[...], bh) + dot(ah[...], bl) + dot(al[...], bh)
        for i in range(NZ):
            for t in range(per):
                o_ref[i, n * per + t] = acc[ROWS * i : ROWS * (i + 1), t * TILE : (t + 1) * TILE]

        @pl.when(n + SLOTS < blocks)
        def _():
            fetch(n + SLOTS).start()

        return carry

    lax.fori_loop(0, blocks, step, 0)


def mm_first_kernel(where_ref, mask_ref, *refs):
    held, b_ref, o_ref, ah, al, slots, sems, stage, row_sems = refs[:-8], *refs[-8:]
    near, late = held[:COLOURS], held[COLOURS:]
    rows = ROWS // 2 // COLOURS
    pieces = [(s, c) for s in range(2 * NZ) for c in range(COLOURS)]

    def copy(i, src):
        return pltpu.make_async_copy(src, stage.at[i], row_sems.at[i])

    for i, (s, c) in enumerate(pieces):
        w = where_ref[c, s]

        @pl.when(w < 8)
        def _(i=i, c=c, w=w):
            copy(i, near[c].at[jnp.minimum(w, 7)]).start()

        @pl.when(w >= 8)
        def _(i=i, c=c, w=w):
            copy(i, late[c].at[jnp.maximum(w - 8, 0)]).start()

    def split_rows():
        for i, (s, c) in enumerate(pieces):
            copy(i, near[c].at[0]).wait()
            hi, lo = split(stage[i])
            at = slice(i * rows, (i + 1) * rows)
            ah[at, :] = hi
            al[at, :] = lo

    mm_body(0, PARTS[0], mask_ref, ah, al, b_ref, o_ref, slots, sems, split_rows)


def mm_next_kernel(mask_ref, ah, al, b_ref, o_ref, slots, sems):
    mm_body(PARTS[0] * TILE // NB, PARTS[1], mask_ref, ah, al, b_ref, o_ref, slots, sems, lambda: None)


SMEM = pl.BlockSpec(memory_space=pltpu.SMEM)
VMEM = pl.BlockSpec(memory_space=pltpu.VMEM)


HBM = pl.BlockSpec(memory_space=pltpu.HBM)


def multiply(kernel, maps, rows, integrals, part, first):
    depth, _ = integrals.shape
    m = NZ * ROWS
    shapes = [jax.ShapeDtypeStruct((NZ, part, ROWS, TILE), f32)]
    scratch = [pltpu.VMEM((SLOTS, depth, NB), f32), pltpu.SemaphoreType.DMA((SLOTS,))]
    if first:
        pieces = 2 * NZ * COLOURS
        shapes += [jax.ShapeDtypeStruct((m, depth), bf16)] * 2
        scratch += [pltpu.VMEM((pieces, m // pieces, depth), f32), pltpu.SemaphoreType.DMA((pieces,))]
    return call(
        kernel,
        tuple(shapes),
        in_specs=[SMEM] * len(maps) + [HBM if first else VMEM] * len(rows) + [HBM],
        out_specs=(VMEM,) * len(shapes),
        scratch_shapes=scratch,
        vmem=40,
        flops=40 * 6 * m * depth * part * TILE,
        nbytes=4 * depth * part * TILE,
    )(*maps, *rows, integrals)


def far_kernel(mine_ref, got_ref, p_ref, m_ref, plus_ref, minus_ref, own_ref):
    half = p_ref.shape[0]
    p_ref[...] = mine_ref[0, :half] + got_ref[0, :half]
    m_ref[...] = mine_ref[0, half:] + got_ref[0, half:]
    plus_ref[...] = mine_ref[1] + got_ref[1]
    minus_ref[...] = mine_ref[2] + got_ref[2]
    own_ref[...] = mine_ref[3] + got_ref[3]


def small(kernel, inputs, shapes, scratch=()):
    shapes = tuple(jax.ShapeDtypeStruct(s, f32) for s in shapes)
    return call(
        kernel,
        shapes,
        in_specs=[SMEM if x.dtype == jnp.int32 else VMEM for x in inputs],
        out_specs=(VMEM,) * len(shapes),
        scratch_shapes=[pltpu.VMEM(s, f32) for s in scratch],
        nbytes=4 * sum(x.size for x in inputs),
    )(*inputs)


def far(mine, got):
    part = mine.shape[1:]
    half = (part[0] // 2, ROWS, TILE)
    return small(far_kernel, (mine, got), (half, half, part, part, part))


def near_kernel(plus_ref, minus_ref, gp_ref, gm_ref, p_ref, m_ref):
    half = gp_ref.shape[0]
    p_ref[:half] = plus_ref[:half] + gp_ref[...]
    p_ref[half:] = plus_ref[half:]
    m_ref[:half] = minus_ref[:half]
    m_ref[half:] = minus_ref[half:] + gm_ref[...]


def near(plus, minus, gp, gm):
    return small(near_kernel, (plus, minus, gp, gm), (plus.shape, plus.shape))


def gather_kernel(idx_ref, *refs):
    ins, (out_ref, scr) = refs[:-2], refs[-2:]
    for p, part in enumerate(PARTS):
        own, rp, rm = ins[3 * p : 3 * p + 3]
        for t in range(part):
            at = (sum(PARTS[:p]) + t) * ROWS
            scr[at : at + ROWS, :] = own[t] + rp[t] + rm[t]

    def step(g, carry):
        for k in range(CAP):
            out_ref[pl.ds(g * CAP + k, 1), :] = scr[pl.ds(idx_ref[g * CAP + k], 1), :]
        return carry

    lax.fori_loop(0, ROWS * TPD // CAP, step, 0)


def gather(idx, parts):
    units = ROWS * TPD
    flat = [x for part in parts for x in part]
    return small(gather_kernel, (idx, *flat), ((units, TILE),), ((units, TILE),))[0]


def finish_kernel(place_ref, got_ref, den_ref, ch_ref, cl_ref, up_ref, ct_ref, scr):
    def step(g, carry):
        for k in range(CAP):
            scr[pl.ds(place_ref[g * CAP + k], 1), :] = got_ref[pl.ds(g * CAP + k, 1), :]
        return carry

    lax.fori_loop(0, ROWS * TPD // CAP, step, 0)
    for t in range(TPD):
        at = slice(t * TILE, (t + 1) * TILE)
        up_ref[:, at] = scr[at, :] / den_ref[:, at]
    dot = functools.partial(jnp.dot, preferred_element_type=f32)
    for k in range(TPD * TILE // RB):
        at = slice(k * RB, (k + 1) * RB)
        hi, lo = split(up_ref[:, at])
        ct_ref[:, at] = dot(hi, ch_ref[at, :]) + dot(hi, cl_ref[at, :]) + dot(lo, ch_ref[at, :])


def finish(place, got, den, ch, cl):
    shape = jax.ShapeDtypeStruct(den.shape, f32)
    whole = lambda s: pl.BlockSpec(s, lambda n: (0, 0))
    return call(
        finish_kernel,
        (shape, shape),
        grid=(1,),
        in_specs=[pl.BlockSpec(memory_space=pltpu.SMEM), whole(got.shape), whole(den.shape), whole(ch.shape), whole(cl.shape)],
        out_specs=(whole(den.shape), whole(den.shape)),
        scratch_shapes=[pltpu.VMEM((ROWS * TPD, TILE), f32)],
        nbytes=8 << 20,
    )(place, got, den, ch, cl)


def plan(destination):
    flat = destination.reshape(-1)
    out_row = flat // VT
    out_tile = flat % VT
    owner = out_row // ROWS * (VT // TPD) + out_tile // TPD
    place = out_tile % TPD * ROWS + out_row % ROWS
    unit = jnp.arange(ROWS * TPD, dtype=jnp.int32)
    row, tile = unit // TPD, unit % TPD
    at = tile * ROWS + row
    key = lax.sort((owner << 22) | (at << 11) | place)
    return (key >> 11) & 2047, key & 2047


def ring(step):
    return [(i, (i + step) % NZ) for i in range(NZ)]


EVEN = [(i, i ^ 1) for i in range(4)]
ODD = [(i, i ^ 3) for i in range(4)]
EXCHANGES = {"xe": ("x", EVEN), "xo": ("x", ODD), "ye": ("y", EVEN), "yo": ("y", ODD)}
ORDERS = [["xe", "xo", "ye", "yo"], ["xo", "ye", "yo", "xe"], ["ye", "yo", "xe", "xo"], ["yo", "xe", "xo", "ye"]]


def exchange(value, name):
    axis, pairs = EXCHANGES[name]
    return lax.ppermute(value, axis, pairs)


def places(ys, xs):
    dx = lax.axis_index("x") ^ xs
    dy = lax.axis_index("y") ^ ys
    bits = {"xe": (dx & 1) ^ (dx >> 1), "xo": dx >> 1, "ye": (dy & 1) ^ (dy >> 1), "yo": dy >> 1}
    return jnp.stack([sum(bits[name] << k for k, name in enumerate(order)) for order in ORDERS])


def after(value, *others):
    return lax.optimization_barrier((value,) + others)[0]


def body(amplitudes, integrals, integral_mask, denominators, cycle_tiles, cycle_mask, destination):
    everyone = ("z", "core", "y", "x")
    z = lax.axis_index("z")
    core = lax.axis_index("core")
    depth = integrals.shape[0]

    towards = jnp.repeat(jnp.array([2, 1, 3, 0], jnp.int32), 2)
    shard = jnp.array([0, 1] * NZ, jnp.int32)
    ys = (z + towards) % NZ
    own = places(ys, 2 * core + shard)
    other = places(ys, 2 * (1 - core) + shard)

    rows = amplitudes.reshape(COLOURS, 1, 64 // COLOURS, depth)
    bufs = [rows[c] for c in range(COLOURS)]

    def exchanged(k):
        got = [exchange(bufs[c], ORDERS[c][k]) for c in range(COLOURS)]
        return got, [jnp.concatenate([b, g], axis=0) for b, g in zip(bufs, got)]

    _, bufs = exchanged(0)
    _, bufs = exchanged(1)
    _, bufs = exchanged(2)
    late = [exchange(bufs[c], ORDERS[c][3]) for c in range(COLOURS)]
    held = (*bufs, *late)

    source, place = plan(after(destination, *bufs))
    place = place.astype(f32).reshape(128, 1, CAP)
    got_place = lax.all_to_all(place, everyone, split_axis=0, concat_axis=0, tiled=True)
    got_place = got_place.reshape(-1).astype(jnp.int32)
    other, got_place, source = lax.optimization_barrier((other, got_place, source))

    def swap(value):
        return lax.ppermute(value, "core", [(0, 1), (1, 0)])

    def along_z(p, m):
        return lax.ppermute(p, "z", ring(1)), lax.ppermute(m, "z", ring(-1))

    def first_product(where):
        return multiply(mm_first_kernel, (where, integral_mask), held, integrals, PARTS[0], True)

    def next_product(mask, hi, lo):
        return multiply(mm_next_kernel, (mask,), (hi, lo), integrals, PARTS[1], False)[0]

    theirs0, other_hi, other_lo = first_product(other)
    from_core0 = swap(theirs0)
    mine0, own_hi, own_lo = first_product(after(own, theirs0))
    p0, m0, plus0, minus0, base0 = far(mine0, from_core0)
    gp0, gm0 = along_z(p0, m0)
    theirs1 = next_product(after(integral_mask, base0), other_hi, other_lo)
    from_core1 = swap(theirs1)
    near0 = near(plus0, minus0, gp0, gm0)
    rp0, rm0 = along_z(*near0)
    mine1 = next_product(after(integral_mask, *near0), own_hi, own_lo)
    p1, m1, plus1, minus1, base1 = far(mine1, from_core1)
    gp1, gm1 = along_z(p1, m1)
    ch, cl = prepare_cycle(after(cycle_tiles, base1), cycle_mask)
    rp1, rm1 = along_z(*near(plus1, minus1, after(gp1, rp0, rm0, ch, cl), gm1))

    sending = gather(source, ((base0, rp0, rm0), (base1, rp1, rm1))).reshape(128, CAP, TILE)
    units = lax.all_to_all(sending, everyone, split_axis=0, concat_axis=0, tiled=True)
    return finish(got_place, units.reshape(-1, TILE), denominators, ch, cl)


def solution(mesh):
    row, col = ("z", "core"), ("y", "x")
    split_mesh = Mesh(mesh.devices.reshape(4, 2, 4, 4), row + col)
    return jax.shard_map(
        body,
        mesh=split_mesh,
        in_specs=(P(col, row), P(row, col), P(row, col), P(row, col), P(col, None), P(col, None), P(row, col)),
        out_specs=(P(row, col), P(row, col)),
        check_vma=False,
    )
```

```python
import functools

import jax
import jax.numpy as jnp
from jax import lax
from jax.experimental import pallas as pl
from jax.experimental.pallas import tpu as pltpu
from jax.sharding import Mesh, PartitionSpec as P

TILE = 128
RB = 512
VT = 256
ROWS = 128
TPD = 16
CAP = 16
NZ = 4
PARTS = (10, 6)
COLOURS = 4
NB = 256
SLOTS = 3
MIB = 1 << 20

f32 = jnp.float32
bf16 = jnp.bfloat16


def split(x):
    hi = x.astype(bf16)
    return hi, (x - hi.astype(f32)).astype(bf16)


def call(kernel, out_shape, *, vmem=16, flops=0, nbytes=0, **kw):
    return pl.pallas_call(
        kernel,
        out_shape=out_shape,
        compiler_params=pltpu.CompilerParams(vmem_limit_bytes=vmem * MIB),
        cost_estimate=pl.CostEstimate(flops=flops, bytes_accessed=nbytes, transcendentals=0),
        **kw,
    )


def masked_split(mask_ref, x_ref, mi, mj, i, j):
    m = mask_ref[mi, mj].astype(f32)
    return split(x_ref[i * TILE : (i + 1) * TILE, j * TILE : (j + 1) * TILE] * m)


def cycle_kernel(mask_ref, x_ref, hi_ref, lo_ref):
    for i in range(RB // TILE):
        for j in range(RB // TILE):
            hi, lo = masked_split(mask_ref, x_ref, pl.program_id(0) * (RB // TILE) + i, j, i, j)
            at = (slice(i * TILE, (i + 1) * TILE), slice(j * TILE, (j + 1) * TILE))
            hi_ref[at] = hi
            lo_ref[at] = lo


def prepare_cycle(x, mask):
    spec = pl.BlockSpec((RB, RB), lambda n: (n, 0))
    out = jax.ShapeDtypeStruct(x.shape, bf16)
    return call(
        cycle_kernel,
        (out, out),
        grid=(x.shape[0] // RB,),
        in_specs=[pl.BlockSpec(memory_space=pltpu.SMEM), spec],
        out_specs=(spec, spec),
        nbytes=x.size * 8,
        flops=x.size * 4,
    )(mask, x)


def integrals_kernel(mask_ref, x_ref, out_ref):
    for i in range(x_ref.shape[0] // TILE):
        for j in range(NB // TILE):
            terms = masked_split(mask_ref, x_ref, i, pl.program_id(0) * (NB // TILE) + j, i, j)
            for k in range(2):
                out_ref[0, k, i * TILE : (i + 1) * TILE, j * TILE : (j + 1) * TILE] = terms[k]


def prepare_integrals(x, mask):
    depth, cols = x.shape
    return call(
        integrals_kernel,
        jax.ShapeDtypeStruct((cols // NB, 2, depth, NB), bf16),
        grid=(cols // NB,),
        in_specs=[pl.BlockSpec(memory_space=pltpu.SMEM), pl.BlockSpec((depth, NB), lambda n: (0, n))],
        out_specs=pl.BlockSpec((1, 2, depth, NB), lambda n: (n, 0, 0, 0)),
        vmem=49,
        nbytes=x.size * 8,
        flops=x.size * 4,
    )(mask, x)


def mm_body(first, tiles_out, ah, al, b_ref, o_ref, slots, sems, before):
    per = NB // TILE
    blocks = tiles_out // per

    def fetch(n):
        slot = n % SLOTS
        return pltpu.make_async_copy(b_ref.at[first + n], slots.at[slot], sems.at[slot])

    for n in range(SLOTS):
        fetch(n).start()
    before()
    dot = functools.partial(jnp.dot, preferred_element_type=f32)

    def step(n, carry):
        fetch(n).wait()
        slot = n % SLOTS
        bh, bl = slots[slot, 0], slots[slot, 1]
        acc = dot(ah[...], bh) + dot(ah[...], bl) + dot(al[...], bh)
        for i in range(NZ):
            for t in range(per):
                o_ref[i, n * per + t] = acc[ROWS * i : ROWS * (i + 1), t * TILE : (t + 1) * TILE]

        @pl.when(n + SLOTS < blocks)
        def _():
            fetch(n + SLOTS).start()

        return carry

    lax.fori_loop(0, blocks, step, 0)


def mm_first_kernel(where_ref, *refs):
    held, b_ref, o_ref, ah, al, slots, sems, stage, row_sems = refs[:-8], *refs[-8:]
    near, late = held[:COLOURS], held[COLOURS:]
    rows = ROWS // 2 // COLOURS
    pieces = [(s, c) for s in range(2 * NZ) for c in range(COLOURS)]

    def copy(i, src):
        return pltpu.make_async_copy(src, stage.at[i], row_sems.at[i])

    for i, (s, c) in enumerate(pieces):
        w = where_ref[c, s]

        @pl.when(w < 8)
        def _(i=i, c=c, w=w):
            copy(i, near[c].at[jnp.minimum(w, 7)]).start()

        @pl.when(w >= 8)
        def _(i=i, c=c, w=w):
            copy(i, late[c].at[jnp.maximum(w - 8, 0)]).start()

    def split_rows():
        for i, (s, c) in enumerate(pieces):
            copy(i, near[c].at[0]).wait()
            hi, lo = split(stage[i])
            at = slice(i * rows, (i + 1) * rows)
            ah[at, :] = hi
            al[at, :] = lo

    mm_body(0, PARTS[0], ah, al, b_ref, o_ref, slots, sems, split_rows)


def mm_next_kernel(ready_ref, ah, al, b_ref, o_ref, slots, sems):
    mm_body(PARTS[0] * TILE // NB, PARTS[1], ah, al, b_ref, o_ref, slots, sems, lambda: None)


SMEM = pl.BlockSpec(memory_space=pltpu.SMEM)
VMEM = pl.BlockSpec(memory_space=pltpu.VMEM)


HBM = pl.BlockSpec(memory_space=pltpu.HBM)


def multiply(kernel, maps, rows, integrals, part, first):
    depth = integrals.shape[2]
    m = NZ * ROWS
    shapes = [jax.ShapeDtypeStruct((NZ, part, ROWS, TILE), f32)]
    scratch = [pltpu.VMEM((SLOTS, 2, depth, NB), bf16), pltpu.SemaphoreType.DMA((SLOTS,))]
    if first:
        pieces = 2 * NZ * COLOURS
        shapes += [jax.ShapeDtypeStruct((m, depth), bf16)] * 2
        scratch += [pltpu.VMEM((pieces, m // pieces, depth), f32), pltpu.SemaphoreType.DMA((pieces,))]
    return call(
        kernel,
        tuple(shapes),
        in_specs=[SMEM] * len(maps) + [HBM if first else VMEM] * len(rows) + [HBM],
        out_specs=(VMEM,) * len(shapes),
        scratch_shapes=scratch,
        vmem=49,
        flops=40 * 6 * m * depth * part * TILE,
        nbytes=4 * depth * part * TILE,
    )(*maps, *rows, integrals)


def far_kernel(mine_ref, got_ref, p_ref, m_ref, plus_ref, minus_ref, own_ref):
    half = p_ref.shape[0]
    p_ref[...] = mine_ref[0, :half] + got_ref[0, :half]
    m_ref[...] = mine_ref[0, half:] + got_ref[0, half:]
    plus_ref[...] = mine_ref[1] + got_ref[1]
    minus_ref[...] = mine_ref[2] + got_ref[2]
    own_ref[...] = mine_ref[3] + got_ref[3]


def small(kernel, inputs, shapes, scratch=()):
    shapes = tuple(jax.ShapeDtypeStruct(s, f32) for s in shapes)
    return call(
        kernel,
        shapes,
        in_specs=[SMEM if x.dtype == jnp.int32 else VMEM for x in inputs],
        out_specs=(VMEM,) * len(shapes),
        scratch_shapes=[pltpu.VMEM(s, f32) for s in scratch],
        nbytes=4 * sum(x.size for x in inputs),
    )(*inputs)


def far(mine, got):
    part = mine.shape[1:]
    half = (part[0] // 2, ROWS, TILE)
    return small(far_kernel, (mine, got), (half, half, part, part, part))


def near_kernel(plus_ref, minus_ref, gp_ref, gm_ref, p_ref, m_ref):
    half = gp_ref.shape[0]
    p_ref[:half] = plus_ref[:half] + gp_ref[...]
    p_ref[half:] = plus_ref[half:]
    m_ref[:half] = minus_ref[:half]
    m_ref[half:] = minus_ref[half:] + gm_ref[...]


def near(plus, minus, gp, gm):
    return small(near_kernel, (plus, minus, gp, gm), (plus.shape, plus.shape))


SLAB = CAP + 1


def gather_kernel(idx_ref, place_ref, *refs):
    ins, (out_ref, scr) = refs[:-2], refs[-2:]
    for p, part in enumerate(PARTS):
        own, rp, rm = ins[3 * p : 3 * p + 3]
        for t in range(part):
            at = (sum(PARTS[:p]) + t) * ROWS
            scr[at : at + ROWS, :] = own[t] + rp[t] + rm[t]

    def step(g, carry):
        for k in range(CAP):
            out_ref[pl.ds(g * SLAB + k, 1), :] = scr[pl.ds(idx_ref[g * CAP + k], 1), :]
        out_ref[pl.ds(g * SLAB + CAP, 1), :] = place_ref[pl.ds(g, 1), :]
        return carry

    lax.fori_loop(0, ROWS * TPD // CAP, step, 0)


def gather(idx, place, parts):
    units = ROWS * TPD
    flat = [x for part in parts for x in part]
    return small(gather_kernel, (idx, place, *flat), ((units // CAP * SLAB, TILE),), ((units, TILE),))[0]


def finish_kernel(got_ref, den_ref, ch_ref, cl_ref, up_ref, ct_ref, scr, place_vec, place_ref, sem):
    peers = ROWS * TPD // CAP
    place_vec[...] = got_ref[pl.ds(CAP, peers, stride=SLAB), :].astype(jnp.int32)
    copy = pltpu.make_async_copy(place_vec, place_ref, sem)
    copy.start()
    copy.wait()

    def step(g, carry):
        for k in range(CAP):
            scr[pl.ds(place_ref[g, k], 1), :] = got_ref[pl.ds(g * SLAB + k, 1), :]
        return carry

    lax.fori_loop(0, peers, step, 0)
    for t in range(TPD):
        at = slice(t * TILE, (t + 1) * TILE)
        up_ref[:, at] = scr[at, :] / den_ref[:, at]
    dot = functools.partial(jnp.dot, preferred_element_type=f32)
    for k in range(TPD * TILE // RB):
        at = slice(k * RB, (k + 1) * RB)
        hi, lo = split(up_ref[:, at])
        ct_ref[:, at] = dot(hi, ch_ref[at, :]) + dot(hi, cl_ref[at, :]) + dot(lo, ch_ref[at, :])


def finish(got, den, ch, cl):
    shape = jax.ShapeDtypeStruct(den.shape, f32)
    peers = ROWS * TPD // CAP
    return call(
        finish_kernel,
        (shape, shape),
        in_specs=[VMEM] * 4,
        out_specs=(VMEM, VMEM),
        scratch_shapes=[
            pltpu.VMEM((ROWS * TPD, TILE), f32),
            pltpu.VMEM((peers, TILE), jnp.int32),
            pltpu.SMEM((peers, TILE), jnp.int32),
            pltpu.SemaphoreType.DMA,
        ],
        nbytes=8 << 20,
    )(got, den, ch, cl)


def plan(destination):
    flat = destination.reshape(-1)
    out_row = flat // VT
    out_tile = flat % VT
    owner = out_row // ROWS * (VT // TPD) + out_tile // TPD
    place = out_tile % TPD * ROWS + out_row % ROWS
    unit = jnp.arange(ROWS * TPD, dtype=jnp.int32)
    row, tile = unit // TPD, unit % TPD
    at = tile * ROWS + row
    key = lax.sort((owner << 22) | (at << 11) | place)
    return (key >> 11) & 2047, key & 2047


def ring(step):
    return [(i, (i + step) % NZ) for i in range(NZ)]


EVEN = [(i, i ^ 1) for i in range(4)]
ODD = [(i, i ^ 3) for i in range(4)]
EXCHANGES = {"xe": ("x", EVEN), "xo": ("x", ODD), "ye": ("y", EVEN), "yo": ("y", ODD)}
ORDERS = [["xe", "xo", "ye", "yo"], ["xo", "ye", "yo", "xe"], ["ye", "yo", "xe", "xo"], ["yo", "xe", "xo", "ye"]]


def exchange(value, name):
    axis, pairs = EXCHANGES[name]
    return lax.ppermute(value, axis, pairs)


def places(ys, xs):
    dx = lax.axis_index("x") ^ xs
    dy = lax.axis_index("y") ^ ys
    bits = {"xe": (dx & 1) ^ (dx >> 1), "xo": dx >> 1, "ye": (dy & 1) ^ (dy >> 1), "yo": dy >> 1}
    return jnp.stack([sum(bits[name] << k for k, name in enumerate(order)) for order in ORDERS])


def after(value, *others):
    return lax.optimization_barrier((value,) + others)[0]


def body(amplitudes, integrals, integral_mask, denominators, cycle_tiles, cycle_mask, destination):
    everyone = ("z", "core", "y", "x")
    z = lax.axis_index("z")
    core = lax.axis_index("core")
    depth = integrals.shape[0]

    towards = jnp.repeat(jnp.array([2, 1, 3, 0], jnp.int32), 2)
    shard = jnp.array([0, 1] * NZ, jnp.int32)
    ys = (z + towards) % NZ
    own = places(ys, 2 * core + shard)
    other = places(ys, 2 * (1 - core) + shard)

    rows = amplitudes.reshape(COLOURS, 1, 64 // COLOURS, depth)
    bufs = [rows[c] for c in range(COLOURS)]

    def exchanged(k):
        got = [exchange(bufs[c], ORDERS[c][k]) for c in range(COLOURS)]
        return got, [jnp.concatenate([b, g], axis=0) for b, g in zip(bufs, got)]

    _, bufs = exchanged(0)
    _, bufs = exchanged(1)
    _, bufs = exchanged(2)
    late = [exchange(bufs[c], ORDERS[c][3]) for c in range(COLOURS)]
    held = (*bufs, *late)

    source, place = plan(after(destination, *bufs))
    place = jnp.pad(place.astype(f32).reshape(128, CAP), ((0, 0), (0, TILE - CAP)))
    terms = prepare_integrals(after(integrals, *bufs), integral_mask)
    other, source, place = lax.optimization_barrier((other, source, place))

    def swap(value):
        return lax.ppermute(value, "core", [(0, 1), (1, 0)])

    def along_z(p, m):
        return lax.ppermute(p, "z", ring(1)), lax.ppermute(m, "z", ring(-1))

    def first_product(where):
        return multiply(mm_first_kernel, (where,), held, terms, PARTS[0], True)

    def next_product(ready, hi, lo):
        return multiply(mm_next_kernel, (ready,), (hi, lo), terms, PARTS[1], False)[0]

    theirs0, other_hi, other_lo = first_product(other)
    from_core0 = swap(theirs0)
    mine0, own_hi, own_lo = first_product(after(own, theirs0))
    p0, m0, plus0, minus0, base0 = far(mine0, from_core0)
    gp0, gm0 = along_z(p0, m0)
    theirs1 = next_product(after(other, base0), other_hi, other_lo)
    from_core1 = swap(theirs1)
    near0 = near(plus0, minus0, gp0, gm0)
    rp0, rm0 = along_z(*near0)
    mine1 = next_product(after(own, *near0), own_hi, own_lo)
    p1, m1, plus1, minus1, base1 = far(mine1, from_core1)
    gp1, gm1 = along_z(p1, m1)
    ch, cl = prepare_cycle(after(cycle_tiles, base1), cycle_mask)
    rp1, rm1 = along_z(*near(plus1, minus1, after(gp1, rp0, rm0, ch, cl), gm1))

    sending = gather(source, place, ((base0, rp0, rm0), (base1, rp1, rm1))).reshape(128, 1, SLAB * TILE)
    units = lax.all_to_all(sending, everyone, split_axis=0, concat_axis=0, tiled=True)
    return finish(units.reshape(-1, TILE), denominators, ch, cl)


def solution(mesh):
    row, col = ("z", "core"), ("y", "x")
    split_mesh = Mesh(mesh.devices.reshape(4, 2, 4, 4), row + col)
    return jax.shard_map(
        body,
        mesh=split_mesh,
        in_specs=(P(col, row), P(row, col), P(row, col), P(row, col), P(col, None), P(col, None), P(row, col)),
        out_specs=(P(row, col), P(row, col)),
        check_vma=False,
    )
```

```python
import functools

import jax
import jax.numpy as jnp
from jax import lax
from jax.experimental import pallas as pl
from jax.experimental.pallas import tpu as pltpu
from jax.sharding import Mesh, PartitionSpec as P

TILE = 128
RB = 512
VT = 256
ROWS = 128
TPD = 16
CAP = 16
NZ = 4
PARTS = (10, 6)
COLOURS = 4
NB = 256
SLOTS = 3
MIB = 1 << 20

f32 = jnp.float32
bf16 = jnp.bfloat16


def split(x):
    hi = x.astype(bf16)
    return hi, (x - hi.astype(f32)).astype(bf16)


def call(kernel, out_shape, *, vmem=16, flops=0, nbytes=0, **kw):
    return pl.pallas_call(
        kernel,
        out_shape=out_shape,
        compiler_params=pltpu.CompilerParams(vmem_limit_bytes=vmem * MIB),
        cost_estimate=pl.CostEstimate(flops=flops, bytes_accessed=nbytes, transcendentals=0),
        **kw,
    )


def masked_split(mask_ref, x_ref, mi, mj, i, j):
    m = mask_ref[mi, mj].astype(f32)
    return split(x_ref[i * TILE : (i + 1) * TILE, j * TILE : (j + 1) * TILE] * m)


def cycle_kernel(mask_ref, x_ref, hi_ref, lo_ref):
    for i in range(RB // TILE):
        for j in range(RB // TILE):
            hi, lo = masked_split(mask_ref, x_ref, pl.program_id(0) * (RB // TILE) + i, j, i, j)
            at = (slice(i * TILE, (i + 1) * TILE), slice(j * TILE, (j + 1) * TILE))
            hi_ref[at] = hi
            lo_ref[at] = lo


def prepare_cycle(x, mask):
    spec = pl.BlockSpec((RB, RB), lambda n: (n, 0))
    out = jax.ShapeDtypeStruct(x.shape, bf16)
    return call(
        cycle_kernel,
        (out, out),
        grid=(x.shape[0] // RB,),
        in_specs=[pl.BlockSpec(memory_space=pltpu.SMEM), spec],
        out_specs=(spec, spec),
        nbytes=x.size * 8,
        flops=x.size * 4,
    )(mask, x)


def integrals_kernel(mask_ref, x_ref, out_ref):
    for i in range(x_ref.shape[0] // TILE):
        for j in range(NB // TILE):
            terms = masked_split(mask_ref, x_ref, i, pl.program_id(0) * (NB // TILE) + j, i, j)
            for k in range(2):
                out_ref[0, k, i * TILE : (i + 1) * TILE, j * TILE : (j + 1) * TILE] = terms[k]


def prepare_integrals(x, mask):
    depth, cols = x.shape
    return call(
        integrals_kernel,
        jax.ShapeDtypeStruct((cols // NB, 2, depth, NB), bf16),
        grid=(cols // NB,),
        in_specs=[pl.BlockSpec(memory_space=pltpu.SMEM), pl.BlockSpec((depth, NB), lambda n: (0, n))],
        out_specs=pl.BlockSpec((1, 2, depth, NB), lambda n: (n, 0, 0, 0)),
        vmem=49,
        nbytes=x.size * 8,
        flops=x.size * 4,
    )(mask, x)


def mm_body(first, tiles_out, ah, al, b_ref, o_ref, slots, sems, before):
    per = NB // TILE
    blocks = tiles_out // per

    def fetch(n):
        slot = n % SLOTS
        return pltpu.make_async_copy(b_ref.at[first + n], slots.at[slot], sems.at[slot])

    for n in range(SLOTS):
        fetch(n).start()
    before()
    dot = functools.partial(jnp.dot, preferred_element_type=f32)

    def step(n, carry):
        fetch(n).wait()
        slot = n % SLOTS
        bh, bl = slots[slot, 0], slots[slot, 1]
        acc = dot(ah[...], bh) + dot(ah[...], bl) + dot(al[...], bh)
        for i in range(NZ):
            for t in range(per):
                o_ref[i, n * per + t] = acc[ROWS * i : ROWS * (i + 1), t * TILE : (t + 1) * TILE]

        @pl.when(n + SLOTS < blocks)
        def _():
            fetch(n + SLOTS).start()

        return carry

    lax.fori_loop(0, blocks, step, 0)


def mm_first_kernel(where_ref, *refs):
    held, b_ref, o_ref, ah, al, slots, sems, stage, row_sems = refs[:-8], *refs[-8:]
    near, late = held[:COLOURS], held[COLOURS:]
    rows = ROWS // 2 // COLOURS
    pieces = [(s, c) for s in range(2 * NZ) for c in range(COLOURS)]

    def copy(i, src):
        return pltpu.make_async_copy(src, stage.at[i], row_sems.at[i])

    for i, (s, c) in enumerate(pieces):
        w = where_ref[c, s]

        @pl.when(w < 8)
        def _(i=i, c=c, w=w):
            copy(i, near[c].at[jnp.minimum(w, 7)]).start()

        @pl.when(w >= 8)
        def _(i=i, c=c, w=w):
            copy(i, late[c].at[jnp.maximum(w - 8, 0)]).start()

    def split_rows():
        for i, (s, c) in enumerate(pieces):
            copy(i, near[c].at[0]).wait()
            hi, lo = split(stage[i])
            at = slice(i * rows, (i + 1) * rows)
            ah[at, :] = hi
            al[at, :] = lo

    mm_body(0, PARTS[0], ah, al, b_ref, o_ref, slots, sems, split_rows)


def mm_next_kernel(ready_ref, ah, al, b_ref, o_ref, slots, sems):
    mm_body(PARTS[0] * TILE // NB, PARTS[1], ah, al, b_ref, o_ref, slots, sems, lambda: None)


SMEM = pl.BlockSpec(memory_space=pltpu.SMEM)
VMEM = pl.BlockSpec(memory_space=pltpu.VMEM)


HBM = pl.BlockSpec(memory_space=pltpu.HBM)


def multiply(kernel, maps, rows, integrals, part, first):
    depth = integrals.shape[2]
    m = NZ * ROWS
    shapes = [jax.ShapeDtypeStruct((NZ, part, ROWS, TILE), f32)]
    scratch = [pltpu.VMEM((SLOTS, 2, depth, NB), bf16), pltpu.SemaphoreType.DMA((SLOTS,))]
    if first:
        pieces = 2 * NZ * COLOURS
        shapes += [jax.ShapeDtypeStruct((m, depth), bf16)] * 2
        scratch += [pltpu.VMEM((pieces, m // pieces, depth), f32), pltpu.SemaphoreType.DMA((pieces,))]
    return call(
        kernel,
        tuple(shapes),
        in_specs=[SMEM] * len(maps) + [HBM if first else VMEM] * len(rows) + [HBM],
        out_specs=(VMEM,) * len(shapes),
        scratch_shapes=scratch,
        vmem=38,
        flops=40 * 6 * m * depth * part * TILE,
        nbytes=4 * depth * part * TILE,
    )(*maps, *rows, integrals)


def far_kernel(mine_ref, got_ref, p_ref, m_ref, plus_ref, minus_ref, own_ref):
    half = p_ref.shape[0]
    p_ref[...] = mine_ref[0, :half] + got_ref[0, :half]
    m_ref[...] = mine_ref[0, half:] + got_ref[0, half:]
    plus_ref[...] = mine_ref[1] + got_ref[1]
    minus_ref[...] = mine_ref[2] + got_ref[2]
    own_ref[...] = mine_ref[3] + got_ref[3]


def small(kernel, inputs, shapes, scratch=()):
    shapes = tuple(jax.ShapeDtypeStruct(s, f32) for s in shapes)
    return call(
        kernel,
        shapes,
        in_specs=[SMEM if x.dtype == jnp.int32 else VMEM for x in inputs],
        out_specs=(VMEM,) * len(shapes),
        scratch_shapes=[pltpu.VMEM(s, f32) for s in scratch],
        nbytes=4 * sum(x.size for x in inputs),
    )(*inputs)


def far(mine, got):
    part = mine.shape[1:]
    half = (part[0] // 2, ROWS, TILE)
    return small(far_kernel, (mine, got), (half, half, part, part, part))


def near_kernel(plus_ref, minus_ref, gp_ref, gm_ref, p_ref, m_ref):
    half = gp_ref.shape[0]
    p_ref[:half] = plus_ref[:half] + gp_ref[...]
    p_ref[half:] = plus_ref[half:]
    m_ref[:half] = minus_ref[:half]
    m_ref[half:] = minus_ref[half:] + gm_ref[...]


def near(plus, minus, gp, gm):
    return small(near_kernel, (plus, minus, gp, gm), (plus.shape, plus.shape))


SLAB = CAP + 1


def gather_kernel(idx_ref, place_ref, *refs):
    ins, (out_ref, scr) = refs[:-2], refs[-2:]
    for p, part in enumerate(PARTS):
        own, rp, rm = ins[3 * p : 3 * p + 3]
        for t in range(part):
            at = (sum(PARTS[:p]) + t) * ROWS
            scr[at : at + ROWS, :] = own[t] + rp[t] + rm[t]

    def step(g, carry):
        for k in range(CAP):
            out_ref[pl.ds(g * SLAB + k, 1), :] = scr[pl.ds(idx_ref[g * CAP + k], 1), :]
        out_ref[pl.ds(g * SLAB + CAP, 1), :] = place_ref[pl.ds(g, 1), :]
        return carry

    lax.fori_loop(0, ROWS * TPD // CAP, step, 0)


def gather(idx, place, parts):
    units = ROWS * TPD
    flat = [x for part in parts for x in part]
    return small(gather_kernel, (idx, place, *flat), ((units // CAP * SLAB, TILE),), ((units, TILE),))[0]


def finish_kernel(got_ref, den_ref, ch_ref, cl_ref, up_ref, ct_ref, scr, place_vec, place_ref, sem):
    peers = ROWS * TPD // CAP
    place_vec[...] = got_ref[pl.ds(CAP, peers, stride=SLAB), :].astype(jnp.int32)
    copy = pltpu.make_async_copy(place_vec, place_ref, sem)
    copy.start()
    copy.wait()

    def step(g, carry):
        for k in range(CAP):
            scr[pl.ds(place_ref[g, k], 1), :] = got_ref[pl.ds(g * SLAB + k, 1), :]
        return carry

    lax.fori_loop(0, peers, step, 0)
    for t in range(TPD):
        at = slice(t * TILE, (t + 1) * TILE)
        up_ref[:, at] = scr[at, :] / den_ref[:, at]
    dot = functools.partial(jnp.dot, preferred_element_type=f32)
    for k in range(TPD * TILE // RB):
        at = slice(k * RB, (k + 1) * RB)
        hi, lo = split(up_ref[:, at])
        ct_ref[:, at] = dot(hi, ch_ref[at, :]) + dot(hi, cl_ref[at, :]) + dot(lo, ch_ref[at, :])


def finish(got, den, ch, cl):
    shape = jax.ShapeDtypeStruct(den.shape, f32)
    peers = ROWS * TPD // CAP
    return call(
        finish_kernel,
        (shape, shape),
        in_specs=[VMEM] * 4,
        out_specs=(VMEM, VMEM),
        scratch_shapes=[
            pltpu.VMEM((ROWS * TPD, TILE), f32),
            pltpu.VMEM((peers, TILE), jnp.int32),
            pltpu.SMEM((peers, TILE), jnp.int32),
            pltpu.SemaphoreType.DMA,
        ],
        nbytes=8 << 20,
    )(got, den, ch, cl)


def plan(destination):
    flat = destination.reshape(-1)
    out_row = flat // VT
    out_tile = flat % VT
    owner = out_row // ROWS * (VT // TPD) + out_tile // TPD
    place = out_tile % TPD * ROWS + out_row % ROWS
    unit = jnp.arange(ROWS * TPD, dtype=jnp.int32)
    row, tile = unit // TPD, unit % TPD
    at = tile * ROWS + row
    key = lax.sort((owner << 22) | (at << 11) | place)
    return (key >> 11) & 2047, key & 2047


def ring(step):
    return [(i, (i + step) % NZ) for i in range(NZ)]


EVEN = [(i, i ^ 1) for i in range(4)]
ODD = [(i, i ^ 3) for i in range(4)]
EXCHANGES = {"xe": ("x", EVEN), "xo": ("x", ODD), "ye": ("y", EVEN), "yo": ("y", ODD)}
ORDERS = [["xe", "xo", "ye", "yo"], ["xo", "ye", "yo", "xe"], ["ye", "yo", "xe", "xo"], ["yo", "xe", "xo", "ye"]]


def exchange(value, name):
    axis, pairs = EXCHANGES[name]
    return lax.ppermute(value, axis, pairs)


def places(ys, xs):
    dx = lax.axis_index("x") ^ xs
    dy = lax.axis_index("y") ^ ys
    bits = {"xe": (dx & 1) ^ (dx >> 1), "xo": dx >> 1, "ye": (dy & 1) ^ (dy >> 1), "yo": dy >> 1}
    return jnp.stack([sum(bits[name] << k for k, name in enumerate(order)) for order in ORDERS])


def after(value, *others):
    return lax.optimization_barrier((value,) + others)[0]


def body(amplitudes, integrals, integral_mask, denominators, cycle_tiles, cycle_mask, destination):
    everyone = ("z", "core", "y", "x")
    z = lax.axis_index("z")
    core = lax.axis_index("core")
    depth = integrals.shape[0]

    towards = jnp.repeat(jnp.array([2, 1, 3, 0], jnp.int32), 2)
    shard = jnp.array([0, 1] * NZ, jnp.int32)
    ys = (z + towards) % NZ
    own = places(ys, 2 * core + shard)
    other = places(ys, 2 * (1 - core) + shard)

    rows = amplitudes.reshape(COLOURS, 1, 64 // COLOURS, depth)
    bufs = [rows[c] for c in range(COLOURS)]

    def exchanged(k):
        got = [exchange(bufs[c], ORDERS[c][k]) for c in range(COLOURS)]
        return got, [jnp.concatenate([b, g], axis=0) for b, g in zip(bufs, got)]

    _, bufs = exchanged(0)
    _, bufs = exchanged(1)
    _, bufs = exchanged(2)
    late = [exchange(bufs[c], ORDERS[c][3]) for c in range(COLOURS)]
    held = (*bufs, *late)

    terms = prepare_integrals(after(integrals, *bufs), integral_mask)

    def swap(value):
        return lax.ppermute(value, "core", [(0, 1), (1, 0)])

    def along_z(p, m):
        return lax.ppermute(p, "z", ring(1)), lax.ppermute(m, "z", ring(-1))

    def first_product(where):
        return multiply(mm_first_kernel, (where,), held, terms, PARTS[0], True)

    def next_product(ready, hi, lo):
        return multiply(mm_next_kernel, (ready,), (hi, lo), terms, PARTS[1], False)[0]

    theirs0, other_hi, other_lo = first_product(other)
    from_core0 = swap(theirs0)
    mine0, own_hi, own_lo = first_product(after(own, theirs0))
    p0, m0, plus0, minus0, base0 = far(mine0, from_core0)
    gp0, gm0 = along_z(p0, m0)
    theirs1 = next_product(after(other, base0), other_hi, other_lo)
    from_core1 = swap(theirs1)
    near0 = near(plus0, minus0, gp0, gm0)
    rp0, rm0 = along_z(*near0)
    mine1 = next_product(after(own, *near0), own_hi, own_lo)
    p1, m1, plus1, minus1, base1 = far(mine1, from_core1)
    gp1, gm1 = along_z(p1, m1)
    ch, cl = prepare_cycle(after(cycle_tiles, base1), cycle_mask)
    near1 = near(plus1, minus1, after(gp1, rp0, rm0, ch, cl), gm1)
    rp1, rm1 = along_z(*near1)

    source, place = plan(after(destination, *near1))
    place = jnp.pad(place.astype(f32).reshape(128, CAP), ((0, 0), (0, TILE - CAP)))

    sending = gather(source, place, ((base0, rp0, rm0), (base1, rp1, rm1))).reshape(128, 1, SLAB * TILE)
    units = lax.all_to_all(sending, everyone, split_axis=0, concat_axis=0, tiled=True)
    return finish(units.reshape(-1, TILE), denominators, ch, cl)


def solution(mesh):
    row, col = ("z", "core"), ("y", "x")
    split_mesh = Mesh(mesh.devices.reshape(4, 2, 4, 4), row + col)
    return jax.shard_map(
        body,
        mesh=split_mesh,
        in_specs=(P(col, row), P(row, col), P(row, col), P(row, col), P(col, None), P(col, None), P(row, col)),
        out_specs=(P(row, col), P(row, col)),
        check_vma=False,
    )
```

```python
import functools

import jax
import jax.numpy as jnp
from jax import lax
from jax.experimental import pallas as pl
from jax.experimental.pallas import tpu as pltpu
from jax.sharding import Mesh, PartitionSpec as P

TILE = 128
RB = 512
VT = 256
ROWS = 128
TPD = 16
CAP = 16
NZ = 4
PARTS = (10, 6)
COLOURS = 4
NB = 256
SLOTS = 3
MIB = 1 << 20

f32 = jnp.float32
bf16 = jnp.bfloat16


def split(x):
    hi = x.astype(bf16)
    return hi, (x - hi.astype(f32)).astype(bf16)


def call(kernel, out_shape, *, vmem=16, flops=0, nbytes=0, **kw):
    return pl.pallas_call(
        kernel,
        out_shape=out_shape,
        compiler_params=pltpu.CompilerParams(vmem_limit_bytes=vmem * MIB),
        cost_estimate=pl.CostEstimate(flops=flops, bytes_accessed=nbytes, transcendentals=0),
        **kw,
    )


def masked_split(mask_ref, x_ref, mi, mj, i, j):
    m = mask_ref[mi, mj].astype(f32)
    return split(x_ref[i * TILE : (i + 1) * TILE, j * TILE : (j + 1) * TILE] * m)


def cycle_kernel(mask_ref, x_ref, hi_ref, lo_ref):
    for i in range(RB // TILE):
        for j in range(RB // TILE):
            hi, lo = masked_split(mask_ref, x_ref, pl.program_id(0) * (RB // TILE) + i, j, i, j)
            at = (slice(i * TILE, (i + 1) * TILE), slice(j * TILE, (j + 1) * TILE))
            hi_ref[at] = hi
            lo_ref[at] = lo


def prepare_cycle(x, mask):
    spec = pl.BlockSpec((RB, RB), lambda n: (n, 0))
    out = jax.ShapeDtypeStruct(x.shape, bf16)
    return call(
        cycle_kernel,
        (out, out),
        grid=(x.shape[0] // RB,),
        in_specs=[pl.BlockSpec(memory_space=pltpu.SMEM), spec],
        out_specs=(spec, spec),
        nbytes=x.size * 8,
        flops=x.size * 4,
    )(mask, x)


def integrals_kernel(mask_ref, x_ref, out_ref):
    for i in range(x_ref.shape[0] // TILE):
        for j in range(NB // TILE):
            terms = masked_split(mask_ref, x_ref, i, pl.program_id(0) * (NB // TILE) + j, i, j)
            for k in range(2):
                out_ref[0, k, i * TILE : (i + 1) * TILE, j * TILE : (j + 1) * TILE] = terms[k]


def prepare_integrals(x, mask):
    depth, cols = x.shape
    return call(
        integrals_kernel,
        jax.ShapeDtypeStruct((cols // NB, 2, depth, NB), bf16),
        grid=(cols // NB,),
        in_specs=[pl.BlockSpec(memory_space=pltpu.SMEM), pl.BlockSpec((depth, NB), lambda n: (0, n))],
        out_specs=pl.BlockSpec((1, 2, depth, NB), lambda n: (n, 0, 0, 0)),
        vmem=49,
        nbytes=x.size * 8,
        flops=x.size * 4,
    )(mask, x)


def mm_body(first, tiles_out, ah, al, b_ref, o_ref, slots, sems, before):
    per = NB // TILE
    blocks = tiles_out // per

    def fetch(n):
        slot = n % SLOTS
        return pltpu.make_async_copy(b_ref.at[first + n], slots.at[slot], sems.at[slot])

    for n in range(SLOTS):
        fetch(n).start()
    before()
    dot = functools.partial(jnp.dot, preferred_element_type=f32)

    def step(n, carry):
        fetch(n).wait()
        slot = n % SLOTS
        bh, bl = slots[slot, 0], slots[slot, 1]
        acc = dot(ah[...], bh) + dot(ah[...], bl) + dot(al[...], bh)
        for i in range(NZ):
            for t in range(per):
                o_ref[i, n * per + t] = acc[ROWS * i : ROWS * (i + 1), t * TILE : (t + 1) * TILE]

        @pl.when(n + SLOTS < blocks)
        def _():
            fetch(n + SLOTS).start()

        return carry

    lax.fori_loop(0, blocks, step, 0)


def mm_first_kernel(where_ref, *refs):
    held, b_ref, o_ref, ah, al, slots, sems, stage, row_sems = refs[:-8], *refs[-8:]
    near, late = held[:COLOURS], held[COLOURS:]
    rows = ROWS // 2 // COLOURS
    pieces = [(s, c) for s in range(2 * NZ) for c in range(COLOURS)]

    def copy(i, src):
        return pltpu.make_async_copy(src, stage.at[i], row_sems.at[i])

    for i, (s, c) in enumerate(pieces):
        w = where_ref[c, s]

        @pl.when(w < 8)
        def _(i=i, c=c, w=w):
            copy(i, near[c].at[jnp.minimum(w, 7)]).start()

        @pl.when(w >= 8)
        def _(i=i, c=c, w=w):
            copy(i, late[c].at[jnp.maximum(w - 8, 0)]).start()

    def split_rows():
        for i, (s, c) in enumerate(pieces):
            copy(i, near[c].at[0]).wait()
            hi, lo = split(stage[i])
            at = slice(i * rows, (i + 1) * rows)
            ah[at, :] = hi
            al[at, :] = lo

    mm_body(0, PARTS[0], ah, al, b_ref, o_ref, slots, sems, split_rows)


def mm_next_kernel(ready_ref, ah, al, b_ref, o_ref, slots, sems):
    mm_body(PARTS[0] * TILE // NB, PARTS[1], ah, al, b_ref, o_ref, slots, sems, lambda: None)


SMEM = pl.BlockSpec(memory_space=pltpu.SMEM)
VMEM = pl.BlockSpec(memory_space=pltpu.VMEM)


HBM = pl.BlockSpec(memory_space=pltpu.HBM)


def multiply(kernel, maps, rows, integrals, part, first):
    depth = integrals.shape[2]
    m = NZ * ROWS
    shapes = [jax.ShapeDtypeStruct((NZ, part, ROWS, TILE), f32)]
    scratch = [pltpu.VMEM((SLOTS, 2, depth, NB), bf16), pltpu.SemaphoreType.DMA((SLOTS,))]
    if first:
        pieces = 2 * NZ * COLOURS
        shapes += [jax.ShapeDtypeStruct((m, depth), bf16)] * 2
        scratch += [pltpu.VMEM((pieces, m // pieces, depth), f32), pltpu.SemaphoreType.DMA((pieces,))]
    return call(
        kernel,
        tuple(shapes),
        in_specs=[SMEM] * len(maps) + [HBM if first else VMEM] * len(rows) + [HBM],
        out_specs=(VMEM,) * len(shapes),
        scratch_shapes=scratch,
        vmem=38,
        flops=40 * 6 * m * depth * part * TILE,
        nbytes=4 * depth * part * TILE,
    )(*maps, *rows, integrals)


def far_kernel(mine_ref, got_ref, p_ref, m_ref, plus_ref, minus_ref, own_ref):
    half = p_ref.shape[0]
    p_ref[...] = mine_ref[0, :half] + got_ref[0, :half]
    m_ref[...] = mine_ref[0, half:] + got_ref[0, half:]
    plus_ref[...] = mine_ref[1] + got_ref[1]
    minus_ref[...] = mine_ref[2] + got_ref[2]
    own_ref[...] = mine_ref[3] + got_ref[3]


def small(kernel, inputs, shapes, scratch=()):
    shapes = tuple(jax.ShapeDtypeStruct(s, f32) for s in shapes)
    return call(
        kernel,
        shapes,
        in_specs=[SMEM if x.dtype == jnp.int32 else VMEM for x in inputs],
        out_specs=(VMEM,) * len(shapes),
        scratch_shapes=[pltpu.VMEM(s, f32) for s in scratch],
        nbytes=4 * sum(x.size for x in inputs),
    )(*inputs)


def far(mine, got):
    part = mine.shape[1:]
    half = (part[0] // 2, ROWS, TILE)
    return small(far_kernel, (mine, got), (half, half, part, part, part))


def near_kernel(plus_ref, minus_ref, gp_ref, gm_ref, p_ref, m_ref):
    half = gp_ref.shape[0]
    p_ref[:half] = plus_ref[:half] + gp_ref[...]
    p_ref[half:] = plus_ref[half:]
    m_ref[:half] = minus_ref[:half]
    m_ref[half:] = minus_ref[half:] + gm_ref[...]


def near(plus, minus, gp, gm):
    return small(near_kernel, (plus, minus, gp, gm), (plus.shape, plus.shape))


SLAB = CAP + 1


def gather_kernel(idx_ref, place_ref, *refs):
    ins, (out_ref, scr) = refs[:-2], refs[-2:]
    for p, part in enumerate(PARTS):
        own, rp, rm = ins[3 * p : 3 * p + 3]
        for t in range(part):
            at = (sum(PARTS[:p]) + t) * ROWS
            scr[at : at + ROWS, :] = own[t] + rp[t] + rm[t]

    def step(g, carry):
        for k in range(CAP):
            out_ref[pl.ds(g * SLAB + k, 1), :] = scr[pl.ds(idx_ref[g * CAP + k], 1), :]
        out_ref[pl.ds(g * SLAB + CAP, 1), :] = place_ref[pl.ds(g, 1), :]
        return carry

    lax.fori_loop(0, ROWS * TPD // CAP, step, 0)


def gather(idx, place, parts):
    units = ROWS * TPD
    flat = [x for part in parts for x in part]
    return small(gather_kernel, (idx, place, *flat), ((units // CAP * SLAB, TILE),), ((units, TILE),))[0]


def finish_kernel(got_ref, den_ref, ch_ref, cl_ref, up_ref, ct_ref, scr, place_vec, place_ref, sem):
    peers = ROWS * TPD // CAP
    place_vec[...] = got_ref[pl.ds(CAP, peers, stride=SLAB), :].astype(jnp.int32)
    copy = pltpu.make_async_copy(place_vec, place_ref, sem)
    copy.start()
    copy.wait()

    def step(g, carry):
        for k in range(CAP):
            scr[pl.ds(place_ref[g, k], 1), :] = got_ref[pl.ds(g * SLAB + k, 1), :]
        return carry

    lax.fori_loop(0, peers, step, 0)
    for t in range(TPD):
        at = slice(t * TILE, (t + 1) * TILE)
        up_ref[:, at] = scr[at, :] / den_ref[:, at]
    dot = functools.partial(jnp.dot, preferred_element_type=f32)
    for k in range(TPD * TILE // RB):
        at = slice(k * RB, (k + 1) * RB)
        hi, lo = split(up_ref[:, at])
        ct_ref[:, at] = dot(hi, ch_ref[at, :]) + dot(hi, cl_ref[at, :]) + dot(lo, ch_ref[at, :])


def finish(got, den, ch, cl):
    shape = jax.ShapeDtypeStruct(den.shape, f32)
    peers = ROWS * TPD // CAP
    return call(
        finish_kernel,
        (shape, shape),
        in_specs=[VMEM] * 4,
        out_specs=(VMEM, VMEM),
        scratch_shapes=[
            pltpu.VMEM((ROWS * TPD, TILE), f32),
            pltpu.VMEM((peers, TILE), jnp.int32),
            pltpu.SMEM((peers, TILE), jnp.int32),
            pltpu.SemaphoreType.DMA,
        ],
        nbytes=8 << 20,
    )(got, den, ch, cl)


def plan(destination):
    flat = destination.reshape(-1)
    out_row = flat // VT
    out_tile = flat % VT
    owner = out_row // ROWS * (VT // TPD) + out_tile // TPD
    place = out_tile % TPD * ROWS + out_row % ROWS
    unit = jnp.arange(ROWS * TPD, dtype=jnp.int32)
    row, tile = unit // TPD, unit % TPD
    at = tile * ROWS + row
    key = lax.sort((owner << 22) | (at << 11) | place)
    return (key >> 11) & 2047, key & 2047


def ring(step):
    return [(i, (i + step) % NZ) for i in range(NZ)]


EVEN = [(i, i ^ 1) for i in range(4)]
ODD = [(i, i ^ 3) for i in range(4)]
EXCHANGES = {"xe": ("x", EVEN), "xo": ("x", ODD), "ye": ("y", EVEN), "yo": ("y", ODD)}
ORDERS = [["xe", "xo", "ye", "yo"], ["xo", "ye", "yo", "xe"], ["ye", "yo", "xe", "xo"], ["yo", "xe", "xo", "ye"]]


def exchange(value, name):
    axis, pairs = EXCHANGES[name]
    return lax.ppermute(value, axis, pairs)


def places(ys, xs):
    dx = lax.axis_index("x") ^ xs
    dy = lax.axis_index("y") ^ ys
    bits = {"xe": (dx & 1) ^ (dx >> 1), "xo": dx >> 1, "ye": (dy & 1) ^ (dy >> 1), "yo": dy >> 1}
    return jnp.stack([sum(bits[name] << k for k, name in enumerate(order)) for order in ORDERS])


def after(value, *others):
    return lax.optimization_barrier((value,) + others)[0]


def body(amplitudes, integrals, integral_mask, denominators, cycle_tiles, cycle_mask, destination):
    everyone = ("z", "core", "y", "x")
    z = lax.axis_index("z")
    core = lax.axis_index("core")
    depth = integrals.shape[0]

    towards = jnp.repeat(jnp.array([2, 1, 3, 0], jnp.int32), 2)
    shard = jnp.array([0, 1] * NZ, jnp.int32)
    ys = (z + towards) % NZ
    own = places(ys, 2 * core + shard)
    other = places(ys, 2 * (1 - core) + shard)

    rows = amplitudes.reshape(COLOURS, 1, 64 // COLOURS, depth)
    bufs = [rows[c] for c in range(COLOURS)]

    def exchanged(k):
        got = [exchange(bufs[c], ORDERS[c][k]) for c in range(COLOURS)]
        return got, [jnp.concatenate([b, g], axis=0) for b, g in zip(bufs, got)]

    _, bufs = exchanged(0)
    _, bufs = exchanged(1)
    _, bufs = exchanged(2)
    late = [exchange(bufs[c], ORDERS[c][3]) for c in range(COLOURS)]
    held = (*bufs, *late)

    source, place = plan(after(destination, *bufs))
    place = jnp.pad(place.astype(f32).reshape(128, CAP), ((0, 0), (0, TILE - CAP)))
    terms = prepare_integrals(after(integrals, *bufs), integral_mask)
    other, source, place = lax.optimization_barrier((other, source, place))

    def swap(value):
        return lax.ppermute(value, "core", [(0, 1), (1, 0)])

    def along_z(p, m):
        return lax.ppermute(p, "z", ring(1)), lax.ppermute(m, "z", ring(-1))

    def first_product(where):
        return multiply(mm_first_kernel, (where,), held, terms, PARTS[0], True)

    def next_product(ready, hi, lo):
        return multiply(mm_next_kernel, (ready,), (hi, lo), terms, PARTS[1], False)[0]

    theirs0, other_hi, other_lo = first_product(other)
    from_core0 = swap(theirs0)
    mine0, own_hi, own_lo = first_product(after(own, theirs0))
    p0, m0, plus0, minus0, base0 = far(mine0, from_core0)
    gp0, gm0 = along_z(p0, m0)
    theirs1 = next_product(after(other, base0), other_hi, other_lo)
    from_core1 = swap(theirs1)
    near0 = near(plus0, minus0, gp0, gm0)
    rp0, rm0 = along_z(*near0)
    mine1 = next_product(after(own, *near0), own_hi, own_lo)
    p1, m1, plus1, minus1, base1 = far(mine1, from_core1)
    gp1, gm1 = along_z(p1, m1)
    ch, cl = prepare_cycle(after(cycle_tiles, base1), cycle_mask)
    rp1, rm1 = along_z(*near(plus1, minus1, after(gp1, rp0, rm0, ch, cl), gm1))

    sending = gather(source, place, ((base0, rp0, rm0), (base1, rp1, rm1))).reshape(128, 1, SLAB * TILE)
    units = lax.all_to_all(sending, everyone, split_axis=0, concat_axis=0, tiled=True)
    return finish(units.reshape(-1, TILE), denominators, ch, cl)


def solution(mesh):
    row, col = ("z", "core"), ("y", "x")
    split_mesh = Mesh(mesh.devices.reshape(4, 2, 4, 4), row + col)
    return jax.shard_map(
        body,
        mesh=split_mesh,
        in_specs=(P(col, row), P(row, col), P(row, col), P(row, col), P(col, None), P(col, None), P(row, col)),
        out_specs=(P(row, col), P(row, col)),
        check_vma=False,
    )
```

```python
import functools

import jax
import jax.numpy as jnp
from jax import lax
from jax.experimental import pallas as pl
from jax.experimental.pallas import tpu as pltpu
from jax.sharding import Mesh, PartitionSpec as P

TILE = 128
RB = 512
VT = 256
ROWS = 128
TPD = 16
CAP = 16
NZ = 4
PARTS = (10, 6)
COLOURS = 4
NB = 256
SLOTS = 2
MIB = 1 << 20

f32 = jnp.float32
bf16 = jnp.bfloat16


def split(x):
    hi = x.astype(bf16)
    return hi, (x - hi.astype(f32)).astype(bf16)


def call(kernel, out_shape, *, vmem=16, flops=0, nbytes=0, **kw):
    return pl.pallas_call(
        kernel,
        out_shape=out_shape,
        compiler_params=pltpu.CompilerParams(vmem_limit_bytes=vmem * MIB),
        cost_estimate=pl.CostEstimate(flops=flops, bytes_accessed=nbytes, transcendentals=0),
        **kw,
    )


def masked_split(mask_ref, x_ref, mi, mj, i, j):
    m = mask_ref[mi, mj].astype(f32)
    return split(x_ref[i * TILE : (i + 1) * TILE, j * TILE : (j + 1) * TILE] * m)


def cycle_kernel(mask_ref, x_ref, hi_ref, lo_ref):
    for i in range(RB // TILE):
        for j in range(RB // TILE):
            hi, lo = masked_split(mask_ref, x_ref, pl.program_id(0) * (RB // TILE) + i, j, i, j)
            at = (slice(i * TILE, (i + 1) * TILE), slice(j * TILE, (j + 1) * TILE))
            hi_ref[at] = hi
            lo_ref[at] = lo


def prepare_cycle(x, mask):
    spec = pl.BlockSpec((RB, RB), lambda n: (n, 0))
    out = jax.ShapeDtypeStruct(x.shape, bf16)
    return call(
        cycle_kernel,
        (out, out),
        grid=(x.shape[0] // RB,),
        in_specs=[pl.BlockSpec(memory_space=pltpu.SMEM), spec],
        out_specs=(spec, spec),
        nbytes=x.size * 8,
        flops=x.size * 4,
    )(mask, x)


def integrals_kernel(mask_ref, x_ref, out_ref):
    for i in range(x_ref.shape[0] // TILE):
        for j in range(NB // TILE):
            terms = masked_split(mask_ref, x_ref, i, pl.program_id(0) * (NB // TILE) + j, i, j)
            for k in range(2):
                out_ref[0, k, i * TILE : (i + 1) * TILE, j * TILE : (j + 1) * TILE] = terms[k]


def prepare_integrals(x, mask):
    depth, cols = x.shape
    return call(
        integrals_kernel,
        jax.ShapeDtypeStruct((cols // NB, 2, depth, NB), bf16),
        grid=(cols // NB,),
        in_specs=[pl.BlockSpec(memory_space=pltpu.SMEM), pl.BlockSpec((depth, NB), lambda n: (0, n))],
        out_specs=pl.BlockSpec((1, 2, depth, NB), lambda n: (n, 0, 0, 0)),
        vmem=56,
        nbytes=x.size * 8,
        flops=x.size * 4,
    )(mask, x)


def mm_body(first, tiles_out, ah, al, b_ref, o_ref, slots, sems, before):
    per = NB // TILE
    blocks = tiles_out // per

    def fetch(n):
        slot = n % SLOTS
        return pltpu.make_async_copy(b_ref.at[first + n], slots.at[slot], sems.at[slot])

    fetch(0).start()
    before()
    dot = functools.partial(jnp.dot, preferred_element_type=f32)

    def step(n, carry):
        fetch(n).wait()

        @pl.when(n + 1 < blocks)
        def _():
            fetch(n + 1).start()

        slot = n % SLOTS
        bh, bl = slots[slot, 0], slots[slot, 1]
        acc = dot(ah[...], bh) + dot(ah[...], bl) + dot(al[...], bh)
        for i in range(NZ):
            for t in range(per):
                o_ref[i, n * per + t] = acc[ROWS * i : ROWS * (i + 1), t * TILE : (t + 1) * TILE]
        return carry

    lax.fori_loop(0, blocks, step, 0)


def mm_first_kernel(where_ref, *refs):
    held, b_ref, o_ref, ah, al, slots, sems, stage, row_sems = refs[:-8], *refs[-8:]
    near, late = held[:COLOURS], held[COLOURS:]
    rows = ROWS // 2 // COLOURS
    pieces = [(s, c) for s in range(2 * NZ) for c in range(COLOURS)]

    def copy(i, src):
        return pltpu.make_async_copy(src, stage.at[i], row_sems.at[i])

    for i, (s, c) in enumerate(pieces):
        w = where_ref[c, s]

        @pl.when(w < 8)
        def _(i=i, c=c, w=w):
            copy(i, near[c].at[jnp.minimum(w, 7)]).start()

        @pl.when(w >= 8)
        def _(i=i, c=c, w=w):
            copy(i, late[c].at[jnp.maximum(w - 8, 0)]).start()

    def split_rows():
        for i, (s, c) in enumerate(pieces):
            copy(i, near[c].at[0]).wait()
            hi, lo = split(stage[i])
            at = slice(i * rows, (i + 1) * rows)
            ah[at, :] = hi
            al[at, :] = lo

    mm_body(0, PARTS[0], ah, al, b_ref, o_ref, slots, sems, split_rows)


def mm_next_kernel(ready_ref, ah, al, b_ref, o_ref, slots, sems):
    mm_body(PARTS[0] * TILE // NB, PARTS[1], ah, al, b_ref, o_ref, slots, sems, lambda: None)


SMEM = pl.BlockSpec(memory_space=pltpu.SMEM)
VMEM = pl.BlockSpec(memory_space=pltpu.VMEM)


HBM = pl.BlockSpec(memory_space=pltpu.HBM)


def multiply(kernel, maps, rows, integrals, part, first):
    depth = integrals.shape[2]
    m = NZ * ROWS
    shapes = [jax.ShapeDtypeStruct((NZ, part, ROWS, TILE), f32)]
    scratch = [pltpu.VMEM((SLOTS, 2, depth, NB), bf16), pltpu.SemaphoreType.DMA((SLOTS,))]
    if first:
        pieces = 2 * NZ * COLOURS
        shapes += [jax.ShapeDtypeStruct((m, depth), bf16)] * 2
        scratch += [pltpu.VMEM((pieces, m // pieces, depth), f32), pltpu.SemaphoreType.DMA((pieces,))]
    return call(
        kernel,
        tuple(shapes),
        in_specs=[SMEM] * len(maps) + [HBM if first else VMEM] * len(rows) + [HBM],
        out_specs=(VMEM,) * len(shapes),
        scratch_shapes=scratch,
        vmem=38,
        flops=40 * 6 * m * depth * part * TILE,
        nbytes=4 * depth * part * TILE,
    )(*maps, *rows, integrals)


def far_kernel(mine_ref, got_ref, p_ref, m_ref, plus_ref, minus_ref, own_ref):
    half = p_ref.shape[0]
    p_ref[...] = mine_ref[0, :half] + got_ref[0, :half]
    m_ref[...] = mine_ref[0, half:] + got_ref[0, half:]
    plus_ref[...] = mine_ref[1] + got_ref[1]
    minus_ref[...] = mine_ref[2] + got_ref[2]
    own_ref[...] = mine_ref[3] + got_ref[3]


def small(kernel, inputs, shapes, scratch=()):
    shapes = tuple(jax.ShapeDtypeStruct(s, f32) for s in shapes)
    return call(
        kernel,
        shapes,
        in_specs=[SMEM if x.dtype == jnp.int32 else VMEM for x in inputs],
        out_specs=(VMEM,) * len(shapes),
        scratch_shapes=[pltpu.VMEM(s, f32) for s in scratch],
        nbytes=4 * sum(x.size for x in inputs),
    )(*inputs)


def far(mine, got):
    part = mine.shape[1:]
    half = (part[0] // 2, ROWS, TILE)
    return small(far_kernel, (mine, got), (half, half, part, part, part))


def near_kernel(plus_ref, minus_ref, gp_ref, gm_ref, p_ref, m_ref):
    half = gp_ref.shape[0]
    p_ref[:half] = plus_ref[:half] + gp_ref[...]
    p_ref[half:] = plus_ref[half:]
    m_ref[:half] = minus_ref[:half]
    m_ref[half:] = minus_ref[half:] + gm_ref[...]


def near(plus, minus, gp, gm):
    return small(near_kernel, (plus, minus, gp, gm), (plus.shape, plus.shape))


SLAB = CAP + 1


def gather_kernel(idx_ref, place_ref, *refs):
    ins, (out_ref, scr) = refs[:-2], refs[-2:]
    for p, part in enumerate(PARTS):
        own, rp, rm = ins[3 * p : 3 * p + 3]
        for t in range(part):
            at = (sum(PARTS[:p]) + t) * ROWS
            scr[at : at + ROWS, :] = own[t] + rp[t] + rm[t]

    def step(g, carry):
        rows = [scr[pl.ds(idx_ref[g * CAP + k], 1), :] for k in range(CAP)]
        for k in range(CAP):
            out_ref[pl.ds(g * SLAB + k, 1), :] = rows[k]
        out_ref[pl.ds(g * SLAB + CAP, 1), :] = place_ref[pl.ds(g, 1), :]
        return carry

    lax.fori_loop(0, ROWS * TPD // CAP, step, 0)


def gather(idx, place, parts):
    units = ROWS * TPD
    flat = [x for part in parts for x in part]
    return small(gather_kernel, (idx, place, *flat), ((units // CAP * SLAB, TILE),), ((units, TILE),))[0]


def finish_kernel(got_ref, den_ref, ch_ref, cl_ref, up_ref, ct_ref, scr, place_vec, place_ref, sem):
    peers = ROWS * TPD // CAP
    place_vec[...] = got_ref[pl.ds(CAP, peers, stride=SLAB), :].astype(jnp.int32)
    copy = pltpu.make_async_copy(place_vec, place_ref, sem)
    copy.start()
    copy.wait()

    def step(g, carry):
        rows = [got_ref[pl.ds(g * SLAB + k, 1), :] for k in range(CAP)]
        for k in range(CAP):
            scr[pl.ds(place_ref[g, k], 1), :] = rows[k]
        return carry

    lax.fori_loop(0, peers, step, 0)
    for t in range(TPD):
        at = slice(t * TILE, (t + 1) * TILE)
        up_ref[:, at] = scr[at, :] / den_ref[:, at]
    dot = functools.partial(jnp.dot, preferred_element_type=f32)
    for k in range(TPD * TILE // RB):
        at = slice(k * RB, (k + 1) * RB)
        hi, lo = split(up_ref[:, at])
        ct_ref[:, at] = dot(hi, ch_ref[at, :]) + dot(hi, cl_ref[at, :]) + dot(lo, ch_ref[at, :])


def finish(got, den, ch, cl):
    shape = jax.ShapeDtypeStruct(den.shape, f32)
    peers = ROWS * TPD // CAP
    return call(
        finish_kernel,
        (shape, shape),
        in_specs=[VMEM] * 4,
        out_specs=(VMEM, VMEM),
        scratch_shapes=[
            pltpu.VMEM((ROWS * TPD, TILE), f32),
            pltpu.VMEM((peers, TILE), jnp.int32),
            pltpu.SMEM((peers, TILE), jnp.int32),
            pltpu.SemaphoreType.DMA,
        ],
        nbytes=8 << 20,
    )(got, den, ch, cl)


def plan(destination):
    flat = destination.reshape(-1)
    out_row = flat // VT
    out_tile = flat % VT
    owner = out_row // ROWS * (VT // TPD) + out_tile // TPD
    place = out_tile % TPD * ROWS + out_row % ROWS
    unit = jnp.arange(ROWS * TPD, dtype=jnp.int32)
    row, tile = unit // TPD, unit % TPD
    at = tile * ROWS + row
    key = lax.sort((owner << 22) | (at << 11) | place)
    return (key >> 11) & 2047, key & 2047


def ring(step):
    return [(i, (i + step) % NZ) for i in range(NZ)]


EVEN = [(i, i ^ 1) for i in range(4)]
ODD = [(i, i ^ 3) for i in range(4)]
EXCHANGES = {"xe": ("x", EVEN), "xo": ("x", ODD), "ye": ("y", EVEN), "yo": ("y", ODD)}
ORDERS = [["xe", "xo", "ye", "yo"], ["xo", "ye", "yo", "xe"], ["ye", "yo", "xe", "xo"], ["yo", "xe", "xo", "ye"]]


def exchange(value, name):
    axis, pairs = EXCHANGES[name]
    return lax.ppermute(value, axis, pairs)


def places(ys, xs):
    dx = lax.axis_index("x") ^ xs
    dy = lax.axis_index("y") ^ ys
    bits = {"xe": (dx & 1) ^ (dx >> 1), "xo": dx >> 1, "ye": (dy & 1) ^ (dy >> 1), "yo": dy >> 1}
    return jnp.stack([sum(bits[name] << k for k, name in enumerate(order)) for order in ORDERS])


def after(value, *others):
    return lax.optimization_barrier((value,) + others)[0]


def body(amplitudes, integrals, integral_mask, denominators, cycle_tiles, cycle_mask, destination):
    everyone = ("z", "core", "y", "x")
    z = lax.axis_index("z")
    core = lax.axis_index("core")
    depth = integrals.shape[0]

    towards = jnp.repeat(jnp.array([2, 1, 3, 0], jnp.int32), 2)
    shard = jnp.array([0, 1] * NZ, jnp.int32)
    ys = (z + towards) % NZ
    own = places(ys, 2 * core + shard)
    other = places(ys, 2 * (1 - core) + shard)

    rows = amplitudes.reshape(COLOURS, 1, 64 // COLOURS, depth)
    bufs = [rows[c] for c in range(COLOURS)]

    def exchanged(k):
        got = [exchange(bufs[c], ORDERS[c][k]) for c in range(COLOURS)]
        return got, [jnp.concatenate([b, g], axis=0) for b, g in zip(bufs, got)]

    _, bufs = exchanged(0)
    _, bufs = exchanged(1)
    _, bufs = exchanged(2)
    late = [exchange(bufs[c], ORDERS[c][3]) for c in range(COLOURS)]
    held = (*bufs, *late)

    source, place = plan(after(destination, *bufs))
    place = jnp.pad(place.astype(f32).reshape(128, CAP), ((0, 0), (0, TILE - CAP)))
    terms = prepare_integrals(after(integrals, *bufs), integral_mask)
    other, source, place = lax.optimization_barrier((other, source, place))

    def swap(value):
        return lax.ppermute(value, "core", [(0, 1), (1, 0)])

    def along_z(p, m):
        return lax.ppermute(p, "z", ring(1)), lax.ppermute(m, "z", ring(-1))

    def first_product(where):
        return multiply(mm_first_kernel, (where,), held, terms, PARTS[0], True)

    def next_product(ready, hi, lo):
        return multiply(mm_next_kernel, (ready,), (hi, lo), terms, PARTS[1], False)[0]

    theirs0, other_hi, other_lo = first_product(other)
    from_core0 = swap(theirs0)
    mine0, own_hi, own_lo = first_product(after(own, theirs0))
    p0, m0, plus0, minus0, base0 = far(mine0, from_core0)
    gp0, gm0 = along_z(p0, m0)
    theirs1 = next_product(after(other, base0), other_hi, other_lo)
    from_core1 = swap(theirs1)
    near0 = near(plus0, minus0, gp0, gm0)
    rp0, rm0 = along_z(*near0)
    mine1 = next_product(after(own, *near0), own_hi, own_lo)
    p1, m1, plus1, minus1, base1 = far(mine1, from_core1)
    gp1, gm1 = along_z(p1, m1)
    ch, cl = prepare_cycle(after(cycle_tiles, base1), cycle_mask)
    rp1, rm1 = along_z(*near(plus1, minus1, after(gp1, rp0, rm0, ch, cl), gm1))

    sending = gather(source, place, ((base0, rp0, rm0), (base1, rp1, rm1))).reshape(128, 1, SLAB * TILE)
    units = lax.all_to_all(sending, everyone, split_axis=0, concat_axis=0, tiled=True)
    return finish(units.reshape(-1, TILE), denominators, ch, cl)


def solution(mesh):
    row, col = ("z", "core"), ("y", "x")
    split_mesh = Mesh(mesh.devices.reshape(4, 2, 4, 4), row + col)
    return jax.shard_map(
        body,
        mesh=split_mesh,
        in_specs=(P(col, row), P(row, col), P(row, col), P(row, col), P(col, None), P(col, None), P(row, col)),
        out_specs=(P(row, col), P(row, col)),
        check_vma=False,
    )
```

```python
import functools

import jax
import jax.numpy as jnp
from jax import lax
from jax.experimental import pallas as pl
from jax.experimental.pallas import tpu as pltpu
from jax.sharding import Mesh, PartitionSpec as P

TILE = 128
RB = 512
VT = 256
ROWS = 128
TPD = 16
CAP = 16
NZ = 4
PARTS = (10, 6)
COLOURS = 4
NB = 256
SLOTS = 2
MIB = 1 << 20

f32 = jnp.float32
bf16 = jnp.bfloat16


def split(x):
    hi = x.astype(bf16)
    return hi, (x - hi.astype(f32)).astype(bf16)


def call(kernel, out_shape, *, vmem=16, flops=0, nbytes=0, **kw):
    return pl.pallas_call(
        kernel,
        out_shape=out_shape,
        compiler_params=pltpu.CompilerParams(vmem_limit_bytes=vmem * MIB),
        cost_estimate=pl.CostEstimate(flops=flops, bytes_accessed=nbytes, transcendentals=0),
        **kw,
    )


def masked_split(mask_ref, x_ref, mi, mj, i, j):
    m = mask_ref[mi, mj].astype(f32)
    return split(x_ref[i * TILE : (i + 1) * TILE, j * TILE : (j + 1) * TILE] * m)


def cycle_kernel(mask_ref, x_ref, hi_ref, lo_ref):
    for i in range(RB // TILE):
        for j in range(RB // TILE):
            hi, lo = masked_split(mask_ref, x_ref, pl.program_id(0) * (RB // TILE) + i, j, i, j)
            at = (slice(i * TILE, (i + 1) * TILE), slice(j * TILE, (j + 1) * TILE))
            hi_ref[at] = hi
            lo_ref[at] = lo


def prepare_cycle(x, mask):
    spec = pl.BlockSpec((RB, RB), lambda n: (n, 0))
    out = jax.ShapeDtypeStruct(x.shape, bf16)
    return call(
        cycle_kernel,
        (out, out),
        grid=(x.shape[0] // RB,),
        in_specs=[pl.BlockSpec(memory_space=pltpu.SMEM), spec],
        out_specs=(spec, spec),
        nbytes=x.size * 8,
        flops=x.size * 4,
    )(mask, x)


def integrals_kernel(mask_ref, x_ref, out_ref):
    for i in range(x_ref.shape[0] // TILE):
        for j in range(NB // TILE):
            terms = masked_split(mask_ref, x_ref, i, pl.program_id(0) * (NB // TILE) + j, i, j)
            for k in range(2):
                out_ref[0, k, i * TILE : (i + 1) * TILE, j * TILE : (j + 1) * TILE] = terms[k]


def prepare_integrals(x, mask):
    depth, cols = x.shape
    return call(
        integrals_kernel,
        jax.ShapeDtypeStruct((cols // NB, 2, depth, NB), bf16),
        grid=(cols // NB,),
        in_specs=[pl.BlockSpec(memory_space=pltpu.SMEM), pl.BlockSpec((depth, NB), lambda n: (0, n))],
        out_specs=pl.BlockSpec((1, 2, depth, NB), lambda n: (n, 0, 0, 0)),
        vmem=56,
        nbytes=x.size * 8,
        flops=x.size * 4,
    )(mask, x)


def mm_body(first, tiles_out, ah, al, b_ref, o_ref, slots, sems, before):
    per = NB // TILE
    blocks = tiles_out // per

    def fetch(n):
        slot = n % SLOTS
        return pltpu.make_async_copy(b_ref.at[first + n], slots.at[slot], sems.at[slot])

    fetch(0).start()
    before()
    dot = functools.partial(jnp.dot, preferred_element_type=f32)

    def step(n, carry):
        fetch(n).wait()

        @pl.when(n + 1 < blocks)
        def _():
            fetch(n + 1).start()

        slot = n % SLOTS
        bh, bl = slots[slot, 0], slots[slot, 1]
        acc = dot(ah[...], bh) + dot(ah[...], bl) + dot(al[...], bh)
        for i in range(NZ):
            for t in range(per):
                o_ref[i, n * per + t] = acc[ROWS * i : ROWS * (i + 1), t * TILE : (t + 1) * TILE]
        return carry

    lax.fori_loop(0, blocks, step, 0)


def mm_first_kernel(where_ref, *refs):
    held, b_ref, o_ref, ah, al, slots, sems, stage, row_sems = refs[:-8], *refs[-8:]
    near, late = held[:COLOURS], held[COLOURS:]
    rows = ROWS // 2 // COLOURS
    pieces = [(s, c) for s in range(2 * NZ) for c in range(COLOURS)]

    def copy(i, src):
        return pltpu.make_async_copy(src, stage.at[i], row_sems.at[i])

    for i, (s, c) in enumerate(pieces):
        w = where_ref[c, s]

        @pl.when(w < 8)
        def _(i=i, c=c, w=w):
            copy(i, near[c].at[jnp.minimum(w, 7)]).start()

        @pl.when(w >= 8)
        def _(i=i, c=c, w=w):
            copy(i, late[c].at[jnp.maximum(w - 8, 0)]).start()

    def split_rows():
        for i, (s, c) in enumerate(pieces):
            copy(i, near[c].at[0]).wait()
            hi, lo = split(stage[i])
            at = slice(i * rows, (i + 1) * rows)
            ah[at, :] = hi
            al[at, :] = lo

    mm_body(0, PARTS[0], ah, al, b_ref, o_ref, slots, sems, split_rows)


def mm_next_kernel(ready_ref, ah, al, b_ref, o_ref, slots, sems):
    mm_body(PARTS[0] * TILE // NB, PARTS[1], ah, al, b_ref, o_ref, slots, sems, lambda: None)


SMEM = pl.BlockSpec(memory_space=pltpu.SMEM)
VMEM = pl.BlockSpec(memory_space=pltpu.VMEM)


HBM = pl.BlockSpec(memory_space=pltpu.HBM)


def multiply(kernel, maps, rows, integrals, part, first):
    depth = integrals.shape[2]
    m = NZ * ROWS
    shapes = [jax.ShapeDtypeStruct((NZ, part, ROWS, TILE), f32)]
    scratch = [pltpu.VMEM((SLOTS, 2, depth, NB), bf16), pltpu.SemaphoreType.DMA((SLOTS,))]
    if first:
        pieces = 2 * NZ * COLOURS
        shapes += [jax.ShapeDtypeStruct((m, depth), bf16)] * 2
        scratch += [pltpu.VMEM((pieces, m // pieces, depth), f32), pltpu.SemaphoreType.DMA((pieces,))]
    return call(
        kernel,
        tuple(shapes),
        in_specs=[SMEM] * len(maps) + [HBM if first else VMEM] * len(rows) + [HBM],
        out_specs=(VMEM,) * len(shapes),
        scratch_shapes=scratch,
        vmem=38,
        flops=40 * 6 * m * depth * part * TILE,
        nbytes=4 * depth * part * TILE,
    )(*maps, *rows, integrals)


def far_kernel(mine_ref, got_ref, p_ref, m_ref):
    half = p_ref.shape[0]
    p_ref[...] = mine_ref[0, :half] + got_ref[0, :half]
    m_ref[...] = mine_ref[0, half:] + got_ref[0, half:]


def small(kernel, inputs, shapes, scratch=()):
    shapes = tuple(jax.ShapeDtypeStruct(s, f32) for s in shapes)
    return call(
        kernel,
        shapes,
        in_specs=[SMEM if x.dtype == jnp.int32 else VMEM for x in inputs],
        out_specs=(VMEM,) * len(shapes),
        scratch_shapes=[pltpu.VMEM(s, f32) for s in scratch],
        nbytes=4 * sum(x.size for x in inputs),
    )(*inputs)


def blocks_of(x, first, count):
    sizes = (count,) + x.shape[1:]
    return pl.BlockSpec(tuple(pl.Element(n) for n in sizes), lambda n: (first, 0, 0, 0))


def whole_of(x):
    return pl.BlockSpec(x.shape, lambda n: (0, 0, 0))


def far(mine, got):
    half = jax.ShapeDtypeStruct((mine.shape[1] // 2, ROWS, TILE), f32)
    return call(
        far_kernel,
        (half, half),
        grid=(1,),
        in_specs=[blocks_of(mine, 0, 1), blocks_of(got, 0, 1)],
        out_specs=(whole_of(half), whole_of(half)),
        nbytes=mine.size * 2,
    )(mine, got)


def near_kernel(mine_ref, got_ref, gp_ref, gm_ref, p_ref, m_ref, own_ref):
    half = gp_ref.shape[0]
    p_ref[:half] = mine_ref[0, :half] + got_ref[0, :half] + gp_ref[...]
    p_ref[half:] = mine_ref[0, half:] + got_ref[0, half:]
    m_ref[:half] = mine_ref[1, :half] + got_ref[1, :half]
    m_ref[half:] = mine_ref[1, half:] + got_ref[1, half:] + gm_ref[...]
    own_ref[...] = mine_ref[2] + got_ref[2]


def near(mine, got, gp, gm):
    part = jax.ShapeDtypeStruct(mine.shape[1:], f32)
    return call(
        near_kernel,
        (part, part, part),
        grid=(1,),
        in_specs=[blocks_of(mine, 1, 3), blocks_of(got, 1, 3), whole_of(gp), whole_of(gm)],
        out_specs=(whole_of(part),) * 3,
        nbytes=mine.size * 8,
    )(mine, got, gp, gm)


SLAB = CAP + 1


def gather_kernel(idx_ref, place_ref, *refs):
    ins, (out_ref, scr) = refs[:-2], refs[-2:]
    for p, part in enumerate(PARTS):
        own, rp, rm = ins[3 * p : 3 * p + 3]
        for t in range(part):
            at = (sum(PARTS[:p]) + t) * ROWS
            scr[at : at + ROWS, :] = own[t] + rp[t] + rm[t]

    def step(g, carry):
        rows = [scr[pl.ds(idx_ref[g * CAP + k], 1), :] for k in range(CAP)]
        for k in range(CAP):
            out_ref[pl.ds(g * SLAB + k, 1), :] = rows[k]
        out_ref[pl.ds(g * SLAB + CAP, 1), :] = place_ref[pl.ds(g, 1), :]
        return carry

    lax.fori_loop(0, ROWS * TPD // CAP, step, 0)


def gather(idx, place, parts):
    units = ROWS * TPD
    flat = [x for part in parts for x in part]
    return small(gather_kernel, (idx, place, *flat), ((units // CAP * SLAB, TILE),), ((units, TILE),))[0]


def finish_kernel(got_ref, den_ref, ch_ref, cl_ref, up_ref, ct_ref, scr, place_vec, place_ref, sem):
    peers = ROWS * TPD // CAP
    place_vec[...] = got_ref[pl.ds(CAP, peers, stride=SLAB), :].astype(jnp.int32)
    copy = pltpu.make_async_copy(place_vec, place_ref, sem)
    copy.start()
    copy.wait()

    def step(g, carry):
        rows = [got_ref[pl.ds(g * SLAB + k, 1), :] for k in range(CAP)]
        for k in range(CAP):
            scr[pl.ds(place_ref[g, k], 1), :] = rows[k]
        return carry

    lax.fori_loop(0, peers, step, 0)
    for t in range(TPD):
        at = slice(t * TILE, (t + 1) * TILE)
        up_ref[:, at] = scr[at, :] / den_ref[:, at]
    dot = functools.partial(jnp.dot, preferred_element_type=f32)
    for k in range(TPD * TILE // RB):
        at = slice(k * RB, (k + 1) * RB)
        hi, lo = split(up_ref[:, at])
        ct_ref[:, at] = dot(hi, ch_ref[at, :]) + dot(hi, cl_ref[at, :]) + dot(lo, ch_ref[at, :])


def finish(got, den, ch, cl):
    shape = jax.ShapeDtypeStruct(den.shape, f32)
    peers = ROWS * TPD // CAP
    return call(
        finish_kernel,
        (shape, shape),
        in_specs=[VMEM] * 4,
        out_specs=(VMEM, VMEM),
        scratch_shapes=[
            pltpu.VMEM((ROWS * TPD, TILE), f32),
            pltpu.VMEM((peers, TILE), jnp.int32),
            pltpu.SMEM((peers, TILE), jnp.int32),
            pltpu.SemaphoreType.DMA,
        ],
        nbytes=8 << 20,
    )(got, den, ch, cl)


def plan(destination):
    flat = destination.reshape(-1)
    out_row = flat // VT
    out_tile = flat % VT
    owner = out_row // ROWS * (VT // TPD) + out_tile // TPD
    place = out_tile % TPD * ROWS + out_row % ROWS
    unit = jnp.arange(ROWS * TPD, dtype=jnp.int32)
    row, tile = unit // TPD, unit % TPD
    at = tile * ROWS + row
    key = lax.sort((owner << 22) | (at << 11) | place)
    return (key >> 11) & 2047, key & 2047


def ring(step):
    return [(i, (i + step) % NZ) for i in range(NZ)]


EVEN = [(i, i ^ 1) for i in range(4)]
ODD = [(i, i ^ 3) for i in range(4)]
EXCHANGES = {"xe": ("x", EVEN), "xo": ("x", ODD), "ye": ("y", EVEN), "yo": ("y", ODD)}
ORDERS = [["xe", "xo", "ye", "yo"], ["xo", "ye", "yo", "xe"], ["ye", "yo", "xe", "xo"], ["yo", "xe", "xo", "ye"]]


def exchange(value, name):
    axis, pairs = EXCHANGES[name]
    return lax.ppermute(value, axis, pairs)


def places(ys, xs):
    dx = lax.axis_index("x") ^ xs
    dy = lax.axis_index("y") ^ ys
    bits = {"xe": (dx & 1) ^ (dx >> 1), "xo": dx >> 1, "ye": (dy & 1) ^ (dy >> 1), "yo": dy >> 1}
    return jnp.stack([sum(bits[name] << k for k, name in enumerate(order)) for order in ORDERS])


def after(value, *others):
    return lax.optimization_barrier((value,) + others)[0]


def body(amplitudes, integrals, integral_mask, denominators, cycle_tiles, cycle_mask, destination):
    everyone = ("z", "core", "y", "x")
    z = lax.axis_index("z")
    core = lax.axis_index("core")
    depth = integrals.shape[0]

    towards = jnp.repeat(jnp.array([2, 1, 3, 0], jnp.int32), 2)
    shard = jnp.array([0, 1] * NZ, jnp.int32)
    ys = (z + towards) % NZ
    own = places(ys, 2 * core + shard)
    other = places(ys, 2 * (1 - core) + shard)

    rows = amplitudes.reshape(COLOURS, 1, 64 // COLOURS, depth)
    bufs = [rows[c] for c in range(COLOURS)]

    def exchanged(k):
        got = [exchange(bufs[c], ORDERS[c][k]) for c in range(COLOURS)]
        return got, [jnp.concatenate([b, g], axis=0) for b, g in zip(bufs, got)]

    _, bufs = exchanged(0)
    _, bufs = exchanged(1)
    _, bufs = exchanged(2)
    late = [exchange(bufs[c], ORDERS[c][3]) for c in range(COLOURS)]
    held = (*bufs, *late)

    source, place = plan(after(destination, *bufs))
    place = jnp.pad(place.astype(f32).reshape(128, CAP), ((0, 0), (0, TILE - CAP)))
    terms = prepare_integrals(after(integrals, *bufs), integral_mask)
    other, source, place = lax.optimization_barrier((other, source, place))

    def swap(value):
        return lax.ppermute(value, "core", [(0, 1), (1, 0)])

    def along_z(p, m):
        return lax.ppermute(p, "z", ring(1)), lax.ppermute(m, "z", ring(-1))

    def first_product(where):
        return multiply(mm_first_kernel, (where,), held, terms, PARTS[0], True)

    def next_product(ready, hi, lo):
        return multiply(mm_next_kernel, (ready,), (hi, lo), terms, PARTS[1], False)[0]

    theirs0, other_hi, other_lo = first_product(other)
    from_core0 = swap(theirs0)
    mine0, own_hi, own_lo = first_product(after(own, theirs0))
    p0, m0 = far(mine0, from_core0)
    gp0, gm0 = along_z(p0, m0)
    theirs1 = next_product(after(other, p0), other_hi, other_lo)
    from_core1 = swap(theirs1)
    near0_p, near0_m, base0 = near(mine0, from_core0, gp0, gm0)
    rp0, rm0 = along_z(near0_p, near0_m)
    mine1 = next_product(after(own, near0_p), own_hi, own_lo)
    p1, m1 = far(mine1, from_core1)
    gp1, gm1 = along_z(p1, m1)
    ch, cl = prepare_cycle(after(cycle_tiles, p1), cycle_mask)
    near1_p, near1_m, base1 = near(mine1, from_core1, after(gp1, rp0, rm0, ch, cl), gm1)
    rp1, rm1 = along_z(near1_p, near1_m)

    sending = gather(source, place, ((base0, rp0, rm0), (base1, rp1, rm1))).reshape(128, 1, SLAB * TILE)
    units = lax.all_to_all(sending, everyone, split_axis=0, concat_axis=0, tiled=True)
    return finish(units.reshape(-1, TILE), denominators, ch, cl)


def solution(mesh):
    row, col = ("z", "core"), ("y", "x")
    split_mesh = Mesh(mesh.devices.reshape(4, 2, 4, 4), row + col)
    return jax.shard_map(
        body,
        mesh=split_mesh,
        in_specs=(P(col, row), P(row, col), P(row, col), P(row, col), P(col, None), P(col, None), P(row, col)),
        out_specs=(P(row, col), P(row, col)),
        check_vma=False,
    )
```
